512 devices in a mesh: row: 32 (over z, core), col: 16 (over y, x).
Axes of the slice: x: 4, y: 4, z: 16, core: 2. Of those that a mesh axis runs over, the one named last changes fastest.
Arguments:
- demo: bfloat16 [32768, 256], P(('row', 'col'))
- rollout: bfloat16 [32768, 256], P(('row', 'col'))
Outputs:
- demo_potential: float32 [32768], P(('row', 'col'))
- rollout_potential: float32 [32768], P(('row', 'col'))
- rollout_reward: float32 [32768], P(('row', 'col'))
All inputs are finite; a program needn't handle non-finite values.
Results may differ from the reference program's by a relative error of at most 0.0065.
The reference program's roundings to bfloat16 on the way (of `demo_unit` and `rollout_unit`) count: a program that leaves them out, or rounds other values in their place, can miss the bound.
Values may be sent and summed in bfloat16 or wider, within the bound.
No kernel may reach another device: no remote copies, remote signals or barrier semaphores. Data moves between devices by JAX's collectives and lax.ppermute only.
A program may use at most 64 MiB of HBM per device.

```python
import math
import jax
import jax.numpy as jnp
from jax import lax

K = 256
ITERS = 2
N = 32768
M = 32768


def shared_parts(key):
    first = jax.random.fold_in(key, 0)
    base = jax.random.normal(first, (N, K), jnp.float32)
    return base


def draw_demo(key, part):
    base = shared_parts(key)
    return base.astype(jnp.bfloat16)


def draw_rollout(key, part):
    base = shared_parts(key)
    key = jax.random.fold_in(key, 23)
    first, second = jax.random.split(key, 2)
    picks = jax.random.randint(first, (M,), 0, N)
    noise = jax.random.normal(second, (M, K), jnp.float32)
    return (base[picks] + 0.6 * noise).astype(jnp.bfloat16)


def setup_inputs(seed: int = 0) -> dict:
    splits = jax.random.split(jax.random.key(seed), 3)
    demo = draw_demo(jax.random.fold_in(splits[2], 71), 0)
    rollout = draw_rollout(jax.random.fold_in(splits[2], 71), 0)
    return {"demo": demo, "rollout": rollout}


EPS = 0.005

def normalize(embed):
    values = embed.astype(jnp.float32)
    inverse = lax.rsqrt(lax.optimization_barrier(jnp.sum(values * values, axis=-1, keepdims=True)) + 1e-06)
    return (values * inverse).astype(jnp.bfloat16)

def cost_of(left, right):
    inner = lax.dot_general(left, right, (((1,), (1,)), ((), ())), preferred_element_type=jnp.float32)
    return 1.0 - inner

def reference(demo, rollout):
    demo_unit = normalize(demo)
    rollout_unit = normalize(rollout)
    total_rows = demo_unit.shape[0]
    total_cols = rollout_unit.shape[0]
    width = demo_unit.shape[1]
    block = min(512, total_rows)
    blocks = demo_unit.reshape(total_rows // block, block, width)
    log_rows = -math.log(total_rows)
    log_cols = -math.log(total_cols)
    g_pot = jnp.zeros((total_cols,), jnp.float32)
    f_pot = jnp.zeros((total_rows,), jnp.float32)
    for step in range(ITERS):

        def row_pass(demo_block):
            tile = cost_of(demo_block, rollout_unit)
            expo = (g_pot[None, :] - tile) / EPS
            top = lax.optimization_barrier(jnp.max(expo, axis=1))
            total = lax.optimization_barrier(jnp.sum(jnp.exp(expo - top[:, None]), axis=1))
            return EPS * log_rows - EPS * (top + jnp.log(total))
        f_pot = lax.map(row_pass, blocks).reshape(total_rows)
        f_blocks = f_pot.reshape(total_rows // block, block)

        def col_step(carry, item):
            top, total = carry
            demo_block, f_part = item
            tile = cost_of(demo_block, rollout_unit)
            expo = (f_part[:, None] - tile) / EPS
            newtop = jnp.maximum(top, lax.optimization_barrier(jnp.max(expo, axis=0)))
            total = total * jnp.exp(top - newtop) + lax.optimization_barrier(jnp.sum(jnp.exp(expo - newtop[None, :]), axis=0))
            return ((newtop, total), None)
        start = (jnp.full((total_cols,), -1e+30, jnp.float32), jnp.zeros((total_cols,), jnp.float32))
        (top, total), unused = lax.scan(col_step, start, (blocks, f_blocks))
        g_pot = EPS * log_cols - EPS * (top + jnp.log(total))
    f_blocks = f_pot.reshape(total_rows // block, block)

    def reward_step(carry, item):
        demo_block, f_part = item
        tile = cost_of(demo_block, rollout_unit)
        plan = jnp.exp((f_part[:, None] + g_pot[None, :] - tile) / EPS)
        return (carry + lax.optimization_barrier(jnp.sum(plan * tile, axis=0)), None)
    weighted, unused = lax.scan(reward_step, jnp.zeros((total_cols,), jnp.float32), (blocks, f_blocks))
    reward = -float(total_cols) * weighted
    return (f_pot / EPS, g_pot / EPS, reward)
```

```python
import functools
import math

import jax
import jax.numpy as jnp
from jax import lax
from jax.experimental import pallas as pl
from jax.experimental.pallas import tpu as pltpu
from jax.sharding import Mesh
from jax.sharding import PartitionSpec as P

EPS = 0.005
SCALE = 1.0 / (EPS * math.log(2.0))
LN2 = math.log(2.0)
LANES = 128
CHUNK = 256
PLANE = ("y", "x")
SHEET = ("core", "y", "x")
LINE = ("zh", "zl")
ALL = ("zh", "zl", "core", "y", "x")
VMEM = pl.BlockSpec(memory_space=pltpu.VMEM)
PARAMS = pltpu.CompilerParams(vmem_limit_bytes=40 * 1024 * 1024)


def normalize(embed):
    values = embed.astype(jnp.float32)
    inverse = lax.rsqrt(jnp.sum(values * values, axis=-1, keepdims=True) + 1e-06)
    return (values * inverse).astype(jnp.bfloat16)


def inner_of(left, right):
    return lax.dot_general(
        left, right, (((1,), (1,)), ((), ())), preferred_element_type=jnp.float32
    )


def log_total(parts):
    top = jnp.max(parts, axis=0)
    return top + jnp.log2(jnp.sum(jnp.exp2(parts - top[None]), axis=0))


def spread_rows(vector, column_ref):
    for block in range(vector.shape[0]):
        wide = jnp.broadcast_to(vector[block : block + 1], (LANES, LANES))
        column_ref[block * LANES : (block + 1) * LANES] = wide.T


def prepare_kernel(demo_ref, rollout_ref, demo_out, rollout_out):
    demo = normalize(demo_ref[...])
    for peer in range(demo_out.shape[0]):
        demo_out[peer] = demo
    rollout = normalize(rollout_ref[...])
    for peer in range(rollout_out.shape[0]):
        rollout_out[peer] = rollout


def row_lse_kernel(
    d0, d1, d2, d3, r0, r1, demo_ref, rollout_ref, out_ref, inner_ref, top_ref
):
    zl = lax.axis_index("zl")
    core = lax.axis_index("core")
    step = d0.shape[0]
    for turn, block in enumerate((d0, d1, d2, d3)):
        at = pl.multiple_of(lax.rem(zl + turn, 4) * step, step)
        demo_ref[pl.ds(at, step)] = block[...]
    half = r0.shape[0]
    rollout_ref[pl.ds(pl.multiple_of(core * half, half), half)] = r0[...]
    rollout_ref[pl.ds(pl.multiple_of((1 - core) * half, half), half)] = r1[...]
    rows = demo_ref.shape[0]
    chunks = rollout_ref.shape[0] // CHUNK
    top_ref[...] = jnp.full_like(top_ref, -4.0)

    def multiply(c, _):
        at = pl.multiple_of(c * CHUNK, CHUNK)
        inner = inner_of(demo_ref[...], rollout_ref[pl.ds(at, CHUNK)])
        inner_ref[c] = inner
        top_ref[...] = jnp.maximum(
            top_ref[...], jnp.maximum(inner[:, :LANES], inner[:, LANES:])
        )
        return 0

    lax.fori_loop(0, chunks, multiply, 0)

    def add_up(b, _):
        at = pl.ds(pl.multiple_of(b * LANES, LANES), LANES)
        top = top_ref[at]
        total = jnp.zeros_like(top)
        for c in range(chunks):
            for lane in (0, LANES):
                entry = inner_ref[c, at, lane : lane + LANES]
                total = total + jnp.exp2((entry - top) * SCALE)
        top, total = top.T, total.T
        peak = jnp.max(top, axis=0, keepdims=True)
        total = jnp.sum(total * jnp.exp2((top - peak) * SCALE), axis=0, keepdims=True)
        line = (peak - 1.0) * SCALE + jnp.log2(total)
        out_ref[:, pl.ds(b, 1)] = jnp.broadcast_to(line[None], (out_ref.shape[0], 1, LANES))
        return 0

    lax.fori_loop(0, rows // LANES, add_up, 0)


def col_lse_kernel(
    log_rows, parts_ref, demo_ref, rollout_ref, phi_ref, out_ref, column_ref, expo_ref, line_ref
):
    phi = -log_rows - log_total(parts_ref[...])
    phi_ref[...] = phi
    spread_rows(phi - SCALE, column_ref)
    rows = demo_ref.shape[0]

    def chunk(c, _):
        at = pl.multiple_of(c * CHUNK, CHUNK)
        inner = inner_of(demo_ref[...], rollout_ref[pl.ds(at, CHUNK)])
        for half in (0, 1):
            expo = inner[:, half * LANES : (half + 1) * LANES] * SCALE + column_ref[...]
            expo_ref[half] = expo
            top = jnp.max(expo.reshape(rows // 8, 8, LANES), axis=0)
            peak = jnp.max(top, axis=0, keepdims=True)
            total = jnp.sum(jnp.exp2(expo_ref[half] - peak), axis=0, keepdims=True)
            line_ref[pl.ds(2 * c + half, 1)] = peak + jnp.log2(total)
        return 0

    lax.fori_loop(0, rollout_ref.shape[0] // CHUNK, chunk, 0)
    out_ref[...] = jnp.broadcast_to(line_ref[...][None], out_ref.shape)


def row_sum_kernel(
    log_cols, parts_ref, phi_ref, demo_ref, rollout_ref, gamma_ref, out_ref, column_ref, total_ref
):
    gamma_ref[...] = -log_cols - log_total(parts_ref[...])
    spread_rows(phi_ref[...] - SCALE, column_ref)
    total_ref[...] = jnp.zeros_like(total_ref)

    def chunk(c, _):
        at = pl.multiple_of(c * CHUNK, CHUNK)
        inner = inner_of(demo_ref[...], rollout_ref[pl.ds(at, CHUNK)])
        column = column_ref[...]
        left = inner[:, :LANES] * SCALE + column + gamma_ref[pl.ds(2 * c, 1)]
        right = inner[:, LANES:] * SCALE + column + gamma_ref[pl.ds(2 * c + 1, 1)]
        total_ref[...] += jnp.exp2(left) + jnp.exp2(right)
        return 0

    lax.fori_loop(0, rollout_ref.shape[0] // CHUNK, chunk, 0)
    for block in range(out_ref.shape[1]):
        total = total_ref[block * LANES : (block + 1) * LANES].T
        line = jnp.sum(total, axis=0, keepdims=True)
        out_ref[:, block : block + 1] = jnp.broadcast_to(
            line[None], (out_ref.shape[0], 1, LANES)
        )


def col_sum_kernel(
    log_rows, parts_ref, phi_ref, gamma_ref, demo_ref, rollout_ref, phi_out, out_ref, column_ref,
    plan_ref, cost_ref
):
    phi = phi_ref[...] - log_rows - jnp.log2(jnp.sum(parts_ref[...], axis=0))
    phi_out[...] = phi
    spread_rows(phi - SCALE, column_ref)

    def chunk(c, _):
        at = pl.multiple_of(c * CHUNK, CHUNK)
        inner = inner_of(demo_ref[...], rollout_ref[pl.ds(at, CHUNK)])
        for half in (0, 1):
            entry = inner[:, half * LANES : (half + 1) * LANES]
            line = pl.ds(2 * c + half, 1)
            plan = jnp.exp2(entry * SCALE + column_ref[...] + gamma_ref[line])
            plan_ref[line] = jnp.sum(plan, axis=0, keepdims=True)
            cost_ref[line] = jnp.sum(plan * (1.0 - entry), axis=0, keepdims=True)
        return 0

    lax.fori_loop(0, rollout_ref.shape[0] // CHUNK, chunk, 0)
    share = LANES // 2
    low = lax.broadcasted_iota(jnp.int32, plan_ref.shape, 1) < share
    plan, cost = plan_ref[...], cost_ref[...]
    even = jnp.where(low, plan, pltpu.roll(cost, share, 1))
    odd = jnp.where(low, pltpu.roll(plan, share, 1), cost)
    for line in range(plan.shape[0]):
        out_ref[2 * line] = even[line : line + 1]
        out_ref[2 * line + 1] = odd[line : line + 1]


def call(kernel, outs, scratch, *args):
    return pl.pallas_call(
        kernel,
        out_shape=outs,
        in_specs=[VMEM] * len(args),
        out_specs=jax.tree.map(lambda _: VMEM, outs),
        scratch_shapes=scratch,
        compiler_params=PARAMS,
    )(*args)


def body(demo, rollout):
    f32, bf16 = jnp.float32, jnp.bfloat16
    shape = jax.ShapeDtypeStruct
    share, width = demo.shape
    n_zh, n_line, n_sheet = lax.axis_size("zh"), lax.axis_size(LINE), lax.axis_size(SHEET)
    n_plane = lax.axis_size(PLANE)
    rows, cols = share * n_line, share * n_sheet
    log_rows, log_cols = math.log2(rows * n_sheet), math.log2(cols * n_line)
    row_vec, col_vec = (rows // LANES, LANES), (cols // LANES, LANES)

    demo_send, rollout_send = call(
        prepare_kernel,
        (shape((n_zh, share, width), bf16), shape((n_plane, share, width), bf16)),
        [],
        demo,
        rollout,
    )
    near = lax.all_to_all(demo_send, "zh", 0, 0, tiled=True).reshape(n_zh * share, width)
    near, rollout_send = lax.optimization_barrier((near, rollout_send))
    n_z = n_line
    blocks = [near]
    for turn in (1, 2, -1):
        blocks.append(lax.ppermute(near, LINE, [((i + turn) % n_z, i) for i in range(n_z)]))
    mine = lax.all_to_all(rollout_send, PLANE, 0, 0, tiled=True).reshape(n_plane * share, width)
    other = lax.ppermute(mine, "core", [(0, 1), (1, 0)])

    demo_unit, rollout_unit, row_parts = call(
        row_lse_kernel,
        (
            shape((rows, width), bf16),
            shape((cols, width), bf16),
            shape((n_line,) + row_vec, f32),
        ),
        [pltpu.VMEM((cols // CHUNK, rows, CHUNK), f32), pltpu.VMEM((rows, LANES), f32)],
        *blocks,
        mine,
        other,
    )
    row_parts = lax.all_to_all(row_parts, LINE, 0, 0, tiled=True)
    phi, col_parts = call(
        functools.partial(col_lse_kernel, log_rows),
        (shape(row_vec, f32), shape((n_sheet,) + col_vec, f32)),
        [pltpu.VMEM((rows, LANES), f32), pltpu.VMEM((2, rows, LANES), f32), pltpu.VMEM(col_vec, f32)],
        row_parts,
        demo_unit,
        rollout_unit,
    )
    col_parts = lax.all_to_all(col_parts, SHEET, 0, 0, tiled=True)
    gamma, row_parts = call(
        functools.partial(row_sum_kernel, log_cols),
        (shape(col_vec, f32), shape((n_line,) + row_vec, f32)),
        [pltpu.VMEM((rows, LANES), f32), pltpu.VMEM((rows, LANES), f32)],
        col_parts,
        phi,
        demo_unit,
        rollout_unit,
    )
    row_parts = lax.all_to_all(row_parts, LINE, 0, 0, tiled=True)
    phi, sums = call(
        functools.partial(col_sum_kernel, log_rows),
        (shape(row_vec, f32), shape((n_sheet, 1, 2 * share), f32)),
        [pltpu.VMEM((rows, LANES), f32), pltpu.VMEM(col_vec, f32), pltpu.VMEM(col_vec, f32)],
        row_parts,
        phi,
        gamma,
        demo_unit,
        rollout_unit,
    )
    sums = lax.all_to_all(sums, SHEET, 0, 0, tiled=True)
    sums = jnp.sum(sums, axis=(0, 1))
    plan, cost = sums[:share], sums[share:]
    at = lax.axis_index(SHEET) * share
    gamma = lax.dynamic_slice_in_dim(gamma.reshape(-1), at, share)
    gamma = gamma - log_cols - jnp.log2(plan)
    reward = -cost / plan
    at = (lax.axis_index("zl") * n_zh + lax.axis_index("zh")) * share
    phi = lax.dynamic_slice_in_dim(phi.reshape(-1), at, share)
    return (phi * LN2, gamma * LN2, reward)


def solution(mesh):
    fine = Mesh(mesh.devices.reshape(4, 4, 2, 4, 4), ALL)
    return jax.shard_map(
        body,
        mesh=fine,
        in_specs=(P(ALL, None), P(ALL, None)),
        out_specs=(P(ALL), P(ALL), P(ALL)),
        check_vma=False,
    )
```

```python
import functools
import math

import jax
import jax.numpy as jnp
from jax import lax
from jax.experimental import pallas as pl
from jax.experimental.pallas import tpu as pltpu
from jax.sharding import Mesh
from jax.sharding import PartitionSpec as P

EPS = 0.005
SCALE = 1.0 / (EPS * math.log(2.0))
LN2 = math.log(2.0)
LANES = 128
CHUNK = 256
PLANE = ("y", "x")
SHEET = ("core", "y", "x")
LINE = ("zh", "zl")
ALL = ("zh", "zl", "core", "y", "x")
VMEM = pl.BlockSpec(memory_space=pltpu.VMEM)
PARAMS = pltpu.CompilerParams(vmem_limit_bytes=6 * 1024 * 1024)


def normalize(embed):
    values = embed.astype(jnp.float32)
    inverse = lax.rsqrt(jnp.sum(values * values, axis=-1, keepdims=True) + 1e-06)
    return (values * inverse).astype(jnp.bfloat16)


def inner_of(left, right):
    return lax.dot_general(
        left, right, (((1,), (1,)), ((), ())), preferred_element_type=jnp.float32
    )


def log_total(parts):
    top = jnp.max(parts, axis=0)
    return top + jnp.log2(jnp.sum(jnp.exp2(parts - top[None]), axis=0))


def spread_rows(vector, column_ref):
    for block in range(vector.shape[0]):
        wide = jnp.broadcast_to(vector[block : block + 1], (LANES, LANES))
        column_ref[block * LANES : (block + 1) * LANES] = wide.T


def block_of(index, size):
    return pl.ds(pl.multiple_of(index * size, size), size)


def prepare_kernel(in_ref, out_ref):
    unit = normalize(in_ref[...])
    for peer in range(out_ref.shape[0]):
        out_ref[peer] = unit


def row_lse_kernel(demo_ref, mine_ref, other_ref, inner_ref, out_ref, top_ref, total_ref):
    core = lax.axis_index("core")
    chunks, rows = inner_ref.shape[:2]
    half = chunks // 2
    top = None
    for side, ref in ((core, mine_ref), (1 - core, other_ref)):
        for c in range(half // 2):
            inner = inner_of(demo_ref[...], ref[c * CHUNK : (c + 1) * CHUNK]) * SCALE
            left, right = inner[:, :LANES], inner[:, LANES:]
            inner_ref[side * half + 2 * c] = left
            inner_ref[side * half + 2 * c + 1] = right
            peak = jnp.maximum(left, right)
            top_ref[...] = peak if top is None else jnp.maximum(top_ref[...], peak)
            top = True

    def add_up(b, _):
        at = block_of(b, 64)
        top = top_ref[at]
        total = jnp.zeros_like(top)
        for c in range(chunks):
            total = total + jnp.exp2(inner_ref[c, at] - top)
        total_ref[at] = total
        return 0

    lax.fori_loop(0, rows // 64, add_up, 0)
    for block in range(rows // LANES):
        at = slice(block * LANES, (block + 1) * LANES)
        top, total = top_ref[at].T, total_ref[at].T
        peak = jnp.max(top, axis=0, keepdims=True)
        total = jnp.sum(total * jnp.exp2(top - peak), axis=0, keepdims=True)
        line = peak - SCALE + jnp.log2(total)
        out_ref[:, block : block + 1] = jnp.broadcast_to(line[None], (out_ref.shape[0], 1, LANES))


def col_lse_kernel(
    log_rows, parts_ref, inner_ref, phi_ref, expo_ref, out_ref, column_ref, line_ref
):
    phi = -log_rows - log_total(parts_ref[...])
    phi_ref[...] = phi
    spread_rows(phi - SCALE, column_ref)
    chunks, rows = inner_ref.shape[:2]
    width = 4

    def group(g, _):
        tops = [None] * width
        for row in range(0, rows, 8):
            at = slice(row, row + 8)
            column = column_ref[at]
            for w in range(width):
                expo = inner_ref[g * width + w, at] + column
                expo_ref[g * width + w, at] = expo
                tops[w] = expo if row == 0 else jnp.maximum(tops[w], expo)
        totals = [jnp.zeros((8, LANES), jnp.float32)] * width
        for row in range(0, rows, 8):
            for w in range(width):
                expo = expo_ref[g * width + w, slice(row, row + 8)]
                totals[w] = totals[w] + jnp.exp2(expo - tops[w])
        for w in range(width):
            peak = jnp.max(tops[w], axis=0, keepdims=True)
            total = jnp.sum(totals[w] * jnp.exp2(tops[w] - peak), axis=0, keepdims=True)
            line_ref[pl.ds(g * width + w, 1)] = peak + jnp.log2(total)
        return 0

    lax.fori_loop(0, chunks // width, group, 0)
    out_ref[...] = jnp.broadcast_to(line_ref[...][None], out_ref.shape)


def row_sum_kernel(log_cols, parts_ref, expo_ref, gamma_ref, plan_ref, out_ref, total_ref):
    gamma = -log_cols - log_total(parts_ref[...])
    gamma_ref[...] = gamma
    chunks, rows = expo_ref.shape[:2]

    def add_up(b, _):
        at = block_of(b, LANES)
        total = jnp.zeros((LANES, LANES), jnp.float32)
        for c in range(chunks):
            plan = jnp.exp2(expo_ref[c, at] + gamma[c : c + 1])
            plan_ref[c, at] = plan
            total = total + plan
        total_ref[at] = total
        return 0

    lax.fori_loop(0, rows // LANES, add_up, 0)
    for block in range(rows // LANES):
        total = total_ref[block * LANES : (block + 1) * LANES].T
        line = jnp.sum(total, axis=0, keepdims=True)
        out_ref[:, block : block + 1] = jnp.broadcast_to(line[None], (out_ref.shape[0], 1, LANES))


def col_sum_kernel(
    log_rows, parts_ref, phi_ref, plan_ref, inner_ref, phi_out, out_ref, column_ref
):
    change = -log_rows - jnp.log2(jnp.sum(parts_ref[...], axis=0))
    phi_out[...] = phi_ref[...] + change
    spread_rows(jnp.exp2(change), column_ref)
    chunks, rows = plan_ref.shape[:2]
    step = 128

    def add_up(b, totals):
        totals = list(totals)
        for row in range(0, step, 8):
            at = pl.ds(pl.multiple_of(b * step + row, 8), 8)
            column = column_ref[at]
            for c in range(chunks):
                plan = plan_ref[c, at] * column
                totals[c] = totals[c] + plan
                totals[chunks + c] = totals[chunks + c] + plan * (SCALE - inner_ref[c, at])
        return tuple(totals)

    zero = jnp.zeros((8, LANES), jnp.float32)
    totals = lax.fori_loop(0, rows // step, add_up, (zero,) * (2 * chunks))
    share = LANES // 2
    low = lax.broadcasted_iota(jnp.int32, (1, LANES), 1) < share
    for c in range(chunks):
        plan = jnp.sum(totals[c], axis=0, keepdims=True)
        cost = jnp.sum(totals[chunks + c], axis=0, keepdims=True) * (1.0 / SCALE)
        out_ref[2 * c] = jnp.where(low, plan, pltpu.roll(cost, share, 1))
        out_ref[2 * c + 1] = jnp.where(low, pltpu.roll(plan, share, 1), cost)


def own_half(ref, index):
    line = ref[pl.ds(lax.div(index, 2), 1)]
    share = LANES // 2
    moved = pltpu.roll(line, share, 1)
    return jnp.where(lax.rem(index, 2) == 0, line, moved)[:, :share]


def finish_kernel(log_cols, ratio, sums_ref, phi_ref, gamma_ref, phi_out, gamma_out, reward_out):
    total = sums_ref[0]
    for peer in range(1, sums_ref.shape[0]):
        total = total + sums_ref[peer]
    share = LANES // 2
    plan, cost = total[:, :share], pltpu.roll(total, share, 1)[:, :share]
    phi_out[...] = own_half(phi_ref, lax.axis_index("zh") * 4 + lax.axis_index("zl")) * LN2
    spot = lax.axis_index("core") * 16 + lax.axis_index("y") * 4 + lax.axis_index("x")
    gamma_out[...] = (own_half(gamma_ref, spot) - log_cols - jnp.log2(plan)) * LN2
    reward_out[...] = -ratio * cost / plan


def call(kernel, outs, scratch, *args):
    return pl.pallas_call(
        kernel,
        out_shape=outs,
        in_specs=[VMEM] * len(args),
        out_specs=jax.tree.map(lambda _: VMEM, outs),
        scratch_shapes=scratch,
        compiler_params=PARAMS,
    )(*args)


def body(demo, rollout):
    f32, bf16 = jnp.float32, jnp.bfloat16
    shape = jax.ShapeDtypeStruct
    share, width = demo.shape
    n_zh, n_line, n_sheet = lax.axis_size("zh"), lax.axis_size(LINE), lax.axis_size(SHEET)
    rows, cols = share * n_line, share * n_sheet
    log_rows, log_cols = math.log2(rows * n_sheet), math.log2(cols * n_line)
    row_vec, col_vec = (rows // LANES, LANES), (cols // LANES, LANES)
    tile = shape((cols // LANES, rows, LANES), f32)
    column = pltpu.VMEM((rows, LANES), f32)

    demo_send = call(prepare_kernel, shape((n_line, share, width), bf16), [], demo)
    rollout_send = call(prepare_kernel, shape((1, share, width), bf16), [], rollout)
    demo_unit = lax.all_to_all(demo_send, LINE, 0, 0, tiled=True).reshape(rows, width)
    mine = lax.all_gather(rollout_send[0], PLANE, axis=0, tiled=True)
    other = lax.ppermute(mine, "core", [(0, 1), (1, 0)])

    inner, row_parts = call(
        row_lse_kernel,
        (tile, shape((n_line,) + row_vec, f32)),
        [column, column],
        demo_unit,
        mine,
        other,
    )
    row_parts = lax.all_to_all(row_parts, LINE, 0, 0, tiled=True)
    phi, expo, col_parts = call(
        functools.partial(col_lse_kernel, log_rows),
        (shape(row_vec, f32), tile, shape((n_sheet,) + col_vec, f32)),
        [column, pltpu.VMEM(col_vec, f32)],
        row_parts,
        inner,
    )
    col_parts = lax.all_to_all(col_parts, SHEET, 0, 0, tiled=True)
    gamma, plan, row_parts = call(
        functools.partial(row_sum_kernel, log_cols),
        (shape(col_vec, f32), tile, shape((n_line,) + row_vec, f32)),
        [column],
        col_parts,
        expo,
    )
    row_parts = lax.all_to_all(row_parts, LINE, 0, 0, tiled=True)
    phi, sums = call(
        functools.partial(col_sum_kernel, log_rows),
        (shape(row_vec, f32), shape((n_sheet, 1, 2 * share), f32)),
        [column],
        row_parts,
        phi,
        plan,
        inner,
    )
    sums = lax.all_to_all(sums, SHEET, 0, 0, tiled=True)
    outs = call(
        functools.partial(finish_kernel, log_cols, 2.0 ** (log_cols - log_rows)),
        (shape((1, share), f32),) * 3,
        [],
        sums,
        phi,
        gamma,
    )
    return tuple(out.reshape(share) for out in outs)


def solution(mesh):
    fine = Mesh(mesh.devices.reshape(4, 4, 2, 4, 4), ALL)
    return jax.shard_map(
        body,
        mesh=fine,
        in_specs=(P(ALL, None), P(ALL, None)),
        out_specs=(P(ALL), P(ALL), P(ALL)),
        check_vma=False,
    )
```

```python
import functools
import math

import jax
import jax.numpy as jnp
from jax import lax
from jax.experimental import pallas as pl
from jax.experimental.pallas import tpu as pltpu
from jax.sharding import Mesh
from jax.sharding import PartitionSpec as P

EPS = 0.005
SCALE = 1.0 / (EPS * math.log(2.0))
LN2 = math.log(2.0)
LANES = 128
CHUNK = 256
PLANE = ("y", "x")
SHEET = ("core", "y", "x")
LINE = ("zh", "zl")
ALL = ("zh", "zl", "core", "y", "x")
VMEM = pl.BlockSpec(memory_space=pltpu.VMEM)
PARAMS = pltpu.CompilerParams(vmem_limit_bytes=6 * 1024 * 1024)


def normalize(embed):
    values = embed.astype(jnp.float32)
    inverse = lax.rsqrt(jnp.sum(values * values, axis=-1, keepdims=True) + 1e-06)
    return (values * inverse).astype(jnp.bfloat16)


def inner_of(left, right):
    return lax.dot_general(
        left, right, (((1,), (1,)), ((), ())), preferred_element_type=jnp.float32
    )


def log_total(parts):
    top = jnp.max(parts, axis=0)
    return top + jnp.log2(jnp.sum(jnp.exp2(parts - top[None]), axis=0))


def spread_rows(vector, column_ref):
    for block in range(vector.shape[0]):
        wide = jnp.broadcast_to(vector[block : block + 1], (LANES, LANES))
        column_ref[block * LANES : (block + 1) * LANES] = wide.T


def prepare_kernel(both_ref, demo_out, rollout_out):
    unit = normalize(both_ref[...])
    share = demo_out.shape[0]
    demo_out[...] = unit[:share]
    for peer in range(rollout_out.shape[0]):
        rollout_out[peer] = unit[share:]


def row_lse_kernel(demo_ref, rollout_ref, inner_ref, out_ref, top_ref, total_ref):
    chunks, rows = inner_ref.shape[:2]
    for c in range(chunks // 2):
        inner = inner_of(demo_ref[...], rollout_ref[c * CHUNK : (c + 1) * CHUNK]) * SCALE
        left, right = inner[:, :LANES], inner[:, LANES:]
        inner_ref[2 * c] = left
        inner_ref[2 * c + 1] = right
        peak = jnp.maximum(left, right)
        top_ref[...] = peak if c == 0 else jnp.maximum(top_ref[...], peak)

    for row in range(0, rows, 64):
        at = slice(row, row + 64)
        top = top_ref[at]
        total = jnp.zeros_like(top)
        for c in range(chunks):
            total = total + jnp.exp2(inner_ref[c, at] - top)
        total_ref[at] = total
    for block in range(rows // LANES):
        at = slice(block * LANES, (block + 1) * LANES)
        top, total = top_ref[at].T, total_ref[at].T
        peak = jnp.max(top, axis=0, keepdims=True)
        total = jnp.sum(total * jnp.exp2(top - peak), axis=0, keepdims=True)
        line = peak - SCALE + jnp.log2(total)
        out_ref[:, block : block + 1] = jnp.broadcast_to(line[None], (out_ref.shape[0], 1, LANES))


def fold(op, values):
    while len(values) > 1:
        values = [op(*pair) for pair in zip(values[::2], values[1::2])]
    return values[0]


def col_lse_kernel(log_rows, parts_ref, inner_ref, phi_ref, column_ref, out_ref, line_ref):
    phi = -log_rows - log_total(parts_ref[...])
    phi_ref[...] = phi
    spread_rows(phi - SCALE, column_ref)
    chunks, rows = inner_ref.shape[:2]
    width, strip, strips = 4, 64, 4

    def group(g, _):
        def some_rows(b, carry):
            tops, totals = list(carry[:width]), list(carry[width:])
            for s in range(strips):
                expos = [[] for _ in range(width)]
                for row in range(0, strip, 8):
                    at = pl.ds(pl.multiple_of((b * strips + s) * strip + row, 8), 8)
                    column = column_ref[at]
                    for w in range(width):
                        expos[w].append(inner_ref[g * width + w, at] + column)
                for w in range(width):
                    top = jnp.maximum(tops[w], fold(jnp.maximum, expos[w]))
                    total = fold(jnp.add, [jnp.exp2(expo - top) for expo in expos[w]])
                    totals[w] = totals[w] * jnp.exp2(tops[w] - top) + total
                    tops[w] = top
            return tuple(tops + totals)

        zero = jnp.zeros((8, LANES), jnp.float32)
        carry = (zero - 1e30,) * width + (zero,) * width
        carry = lax.fori_loop(0, rows // (strip * strips), some_rows, carry)
        for w in range(width):
            peak = jnp.max(carry[w], axis=0, keepdims=True)
            total = carry[width + w] * jnp.exp2(carry[w] - peak)
            total = jnp.sum(total, axis=0, keepdims=True)
            line_ref[pl.ds(g * width + w, 1)] = peak + jnp.log2(total)
        return 0

    lax.fori_loop(0, chunks // width, group, 0)
    out_ref[...] = jnp.broadcast_to(line_ref[...][None], out_ref.shape)


def row_sum_kernel(
    log_cols, parts_ref, column_ref, inner_ref, gamma_ref, plan_ref, out_ref, total_ref
):
    gamma = -log_cols - log_total(parts_ref[...])
    gamma_ref[...] = gamma
    chunks, rows = inner_ref.shape[:2]
    for row in range(0, rows, LANES):
        at = slice(row, row + LANES)
        column = column_ref[at]
        total = jnp.zeros_like(column)
        for c in range(chunks):
            plan = jnp.exp2(inner_ref[c, at] + (column + gamma[c : c + 1]))
            plan_ref[c, at] = plan
            total = total + plan
        total_ref[at] = total
    for block in range(rows // LANES):
        total = total_ref[block * LANES : (block + 1) * LANES].T
        line = jnp.sum(total, axis=0, keepdims=True)
        out_ref[:, block : block + 1] = jnp.broadcast_to(line[None], (out_ref.shape[0], 1, LANES))


def col_sum_kernel(
    log_rows, parts_ref, phi_ref, plan_ref, inner_ref, phi_out, out_ref, column_ref
):
    change = -log_rows - jnp.log2(jnp.sum(parts_ref[...], axis=0))
    phi_out[...] = phi_ref[...] + change
    spread_rows(jnp.exp2(change), column_ref)
    chunks, rows = plan_ref.shape[:2]
    step = 128

    def add_up(b, totals):
        totals = list(totals)
        for row in range(0, step, 8):
            at = pl.ds(pl.multiple_of(b * step + row, 8), 8)
            column = column_ref[at]
            for c in range(chunks):
                plan = plan_ref[c, at] * column
                totals[c] = totals[c] + plan
                totals[chunks + c] = totals[chunks + c] + plan * (SCALE - inner_ref[c, at])
        return tuple(totals)

    zero = jnp.zeros((8, LANES), jnp.float32)
    totals = lax.fori_loop(0, rows // step, add_up, (zero,) * (2 * chunks), unroll=2)
    share = LANES // 2
    low = lax.broadcasted_iota(jnp.int32, (1, LANES), 1) < share
    for c in range(chunks):
        plan = jnp.sum(totals[c], axis=0, keepdims=True)
        cost = jnp.sum(totals[chunks + c], axis=0, keepdims=True) * (1.0 / SCALE)
        out_ref[2 * c] = jnp.where(low, plan, pltpu.roll(cost, share, 1))
        out_ref[2 * c + 1] = jnp.where(low, pltpu.roll(plan, share, 1), cost)


def own_half(ref, index):
    line = ref[pl.ds(lax.div(index, 2), 1)]
    share = LANES // 2
    moved = pltpu.roll(line, share, 1)
    return jnp.where(lax.rem(index, 2) == 0, line, moved)[:, :share]


def finish_kernel(log_cols, ratio, sums_ref, phi_ref, gamma_ref, phi_out, gamma_out, reward_out):
    total = sums_ref[0]
    for peer in range(1, sums_ref.shape[0]):
        total = total + sums_ref[peer]
    share = LANES // 2
    plan, cost = total[:, :share], pltpu.roll(total, share, 1)[:, :share]
    phi_out[...] = own_half(phi_ref, lax.axis_index("zh") * 4 + lax.axis_index("zl")) * LN2
    spot = lax.axis_index("core") * 16 + lax.axis_index("y") * 4 + lax.axis_index("x")
    gamma_out[...] = (own_half(gamma_ref, spot) - log_cols - jnp.log2(plan)) * LN2
    reward_out[...] = -ratio * cost / plan


def call(kernel, outs, scratch, *args):
    return pl.pallas_call(
        kernel,
        out_shape=outs,
        in_specs=[VMEM] * len(args),
        out_specs=jax.tree.map(lambda _: VMEM, outs),
        scratch_shapes=scratch,
        compiler_params=PARAMS,
    )(*args)


def body(demo, rollout):
    f32, bf16 = jnp.float32, jnp.bfloat16
    shape = jax.ShapeDtypeStruct
    share, width = demo.shape
    n_zh, n_line, n_sheet = lax.axis_size("zh"), lax.axis_size(LINE), lax.axis_size(SHEET)
    rows, cols = share * n_line, share * n_sheet
    log_rows, log_cols = math.log2(rows * n_sheet), math.log2(cols * n_line)
    row_vec, col_vec = (rows // LANES, LANES), (cols // LANES, LANES)
    tile = shape((cols // LANES, rows, LANES), f32)
    column = pltpu.VMEM((rows, LANES), f32)

    both = lax.optimization_barrier(jnp.concatenate([demo, rollout]))
    demo_send, rollout_send = call(
        prepare_kernel,
        (shape((share, width), bf16), shape((n_sheet, share, width), bf16)),
        [],
        both,
    )
    rollout_unit = lax.all_to_all(rollout_send, SHEET, 0, 0, tiled=True).reshape(cols, width)
    demo_unit = lax.all_gather(demo_send, LINE, axis=0, tiled=True)

    inner, row_parts = call(
        row_lse_kernel,
        (tile, shape((n_line,) + row_vec, f32)),
        [column, column],
        demo_unit,
        rollout_unit,
    )
    row_parts = lax.all_to_all(row_parts, LINE, 0, 0, tiled=True)
    phi, spread, col_parts = call(
        functools.partial(col_lse_kernel, log_rows),
        (shape(row_vec, f32), shape((rows, LANES), f32), shape((n_sheet,) + col_vec, f32)),
        [pltpu.VMEM(col_vec, f32)],
        row_parts,
        inner,
    )
    col_parts = lax.all_to_all(col_parts, SHEET, 0, 0, tiled=True)
    gamma, plan, row_parts = call(
        functools.partial(row_sum_kernel, log_cols),
        (shape(col_vec, f32), tile, shape((n_line,) + row_vec, f32)),
        [column],
        col_parts,
        spread,
        inner,
    )
    row_parts = lax.all_to_all(row_parts, LINE, 0, 0, tiled=True)
    phi, sums = call(
        functools.partial(col_sum_kernel, log_rows),
        (shape(row_vec, f32), shape((n_sheet, 1, 2 * share), f32)),
        [column],
        row_parts,
        phi,
        plan,
        inner,
    )
    sums = lax.all_to_all(sums, SHEET, 0, 0, tiled=True)
    outs = call(
        functools.partial(finish_kernel, log_cols, 2.0 ** (log_cols - log_rows)),
        (shape((1, share), f32),) * 3,
        [],
        sums,
        phi,
        gamma,
    )
    return tuple(out.reshape(share) for out in outs)


def solution(mesh):
    fine = Mesh(mesh.devices.reshape(4, 4, 2, 4, 4), ALL)
    return jax.shard_map(
        body,
        mesh=fine,
        in_specs=(P(ALL, None), P(ALL, None)),
        out_specs=(P(ALL), P(ALL), P(ALL)),
        check_vma=False,
    )
```

```python
import functools
import math

import jax
import jax.numpy as jnp
from jax import lax
from jax.experimental import pallas as pl
from jax.experimental.pallas import tpu as pltpu
from jax.sharding import Mesh
from jax.sharding import PartitionSpec as P

EPS = 0.005
SCALE = 1.0 / (EPS * math.log(2.0))
LN2 = math.log(2.0)
LANES = 128
CHUNK = 256
PLANE = ("y", "x")
SHEET = ("core", "y", "x")
LINE = ("zh", "zl")
ROW = ("zh", "zl", "core")
TURNS = [[2 * z + (z + turn) % 2 for z in range(16)] for turn in (0, 1)]
ALL = ("zh", "zl", "core", "y", "x")
VMEM = pl.BlockSpec(memory_space=pltpu.VMEM)
PARAMS = pltpu.CompilerParams(vmem_limit_bytes=6 * 1024 * 1024)


def normalize(embed):
    values = embed.astype(jnp.float32)
    inverse = lax.rsqrt(jnp.sum(values * values, axis=-1, keepdims=True) + 1e-06)
    return (values * inverse).astype(jnp.bfloat16)


def inner_of(left, right):
    return lax.dot_general(
        left, right, (((1,), (1,)), ((), ())), preferred_element_type=jnp.float32
    )


def log_total(parts):
    top = jnp.max(parts, axis=0)
    return top + jnp.log2(jnp.sum(jnp.exp2(parts - top[None]), axis=0))


def spread_rows(vector, column_ref):
    for block in range(vector.shape[0]):
        wide = jnp.broadcast_to(vector[block : block + 1], (LANES, LANES))
        column_ref[block * LANES : (block + 1) * LANES] = wide.T


def prepare_kernel(both_ref, demo_out, rollout_out):
    unit = normalize(both_ref[...])
    share = demo_out.shape[0]
    demo_out[...] = unit[:share]
    for peer in range(rollout_out.shape[0]):
        rollout_out[peer] = unit[share:]


def row_lse_kernel(demo_ref, rollout_ref, inner_ref, out_ref, top_ref, total_ref):
    chunks, rows = inner_ref.shape[:2]
    for c in range(chunks // 2):
        inner = inner_of(demo_ref[...], rollout_ref[c * CHUNK : (c + 1) * CHUNK]) * SCALE
        left, right = inner[:, :LANES], inner[:, LANES:]
        inner_ref[2 * c] = left
        inner_ref[2 * c + 1] = right
        peak = jnp.maximum(left, right)
        top_ref[...] = peak if c == 0 else jnp.maximum(top_ref[...], peak)

    for row in range(0, rows, 64):
        at = slice(row, row + 64)
        top = top_ref[at]
        total = jnp.zeros_like(top)
        for c in range(chunks):
            total = total + jnp.exp2(inner_ref[c, at] - top)
        total_ref[at] = total
    for block in range(rows // LANES):
        at = slice(block * LANES, (block + 1) * LANES)
        top, total = top_ref[at].T, total_ref[at].T
        peak = jnp.max(top, axis=0, keepdims=True)
        total = jnp.sum(total * jnp.exp2(top - peak), axis=0, keepdims=True)
        line = peak - SCALE + jnp.log2(total)
        out_ref[:, block : block + 1] = jnp.broadcast_to(line[None], (out_ref.shape[0], 1, LANES))


def fold(op, values):
    while len(values) > 1:
        values = [op(*pair) for pair in zip(values[::2], values[1::2])]
    return values[0]


def col_lse_kernel(log_rows, parts_ref, inner_ref, phi_ref, column_ref, out_ref, line_ref):
    phi = -log_rows - log_total(parts_ref[...])
    phi_ref[...] = phi
    spread_rows(phi - SCALE, column_ref)
    chunks, rows = inner_ref.shape[:2]
    width, strip, strips = 4, 64, 4

    def group(g, _):
        def some_rows(b, carry):
            tops, totals = list(carry[:width]), list(carry[width:])
            for s in range(strips):
                expos = [[] for _ in range(width)]
                for row in range(0, strip, 8):
                    at = pl.ds(pl.multiple_of((b * strips + s) * strip + row, 8), 8)
                    column = column_ref[at]
                    for w in range(width):
                        expos[w].append(inner_ref[g * width + w, at] + column)
                for w in range(width):
                    top = jnp.maximum(tops[w], fold(jnp.maximum, expos[w]))
                    total = fold(jnp.add, [jnp.exp2(expo - top) for expo in expos[w]])
                    totals[w] = totals[w] * jnp.exp2(tops[w] - top) + total
                    tops[w] = top
            return tuple(tops + totals)

        zero = jnp.zeros((8, LANES), jnp.float32)
        carry = (zero - 1e30,) * width + (zero,) * width
        carry = lax.fori_loop(0, rows // (strip * strips), some_rows, carry)
        for w in range(width):
            peak = jnp.max(carry[w], axis=0, keepdims=True)
            total = carry[width + w] * jnp.exp2(carry[w] - peak)
            total = jnp.sum(total, axis=0, keepdims=True)
            line_ref[pl.ds(g * width + w, 1)] = peak + jnp.log2(total)
        return 0

    lax.fori_loop(0, chunks // width, group, 0)
    out_ref[...] = jnp.broadcast_to(line_ref[...][None], out_ref.shape)


def row_sum_kernel(
    log_cols, parts_ref, column_ref, inner_ref, gamma_ref, plan_ref, out_ref, total_ref
):
    gamma = -log_cols - log_total(parts_ref[...])
    gamma_ref[...] = gamma
    chunks, rows = inner_ref.shape[:2]
    for row in range(0, rows, LANES):
        at = slice(row, row + LANES)
        column = column_ref[at]
        total = jnp.zeros_like(column)
        for c in range(chunks):
            plan = jnp.exp2(inner_ref[c, at] + (column + gamma[c : c + 1]))
            plan_ref[c, at] = plan
            total = total + plan
        total_ref[at] = total
    for block in range(rows // LANES):
        total = total_ref[block * LANES : (block + 1) * LANES].T
        line = jnp.sum(total, axis=0, keepdims=True)
        out_ref[:, block : block + 1] = jnp.broadcast_to(line[None], (out_ref.shape[0], 1, LANES))


def col_sum_kernel(
    log_rows, parts_ref, phi_ref, plan_ref, inner_ref, phi_out, out_ref, column_ref
):
    change = -log_rows - jnp.log2(jnp.sum(parts_ref[...], axis=0))
    phi_out[...] = phi_ref[...] + change
    spread_rows(jnp.exp2(change), column_ref)
    chunks, rows = plan_ref.shape[:2]
    step = 128

    def add_up(b, totals):
        totals = list(totals)
        for row in range(0, step, 8):
            at = pl.ds(pl.multiple_of(b * step + row, 8), 8)
            column = column_ref[at]
            for c in range(chunks):
                plan = plan_ref[c, at] * column
                totals[c] = totals[c] + plan
                totals[chunks + c] = totals[chunks + c] + plan * (SCALE - inner_ref[c, at])
        return tuple(totals)

    zero = jnp.zeros((8, LANES), jnp.float32)
    totals = lax.fori_loop(0, rows // step, add_up, (zero,) * (2 * chunks), unroll=2)
    share = LANES // 2
    low = lax.broadcasted_iota(jnp.int32, (1, LANES), 1) < share
    for c in range(chunks):
        plan = jnp.sum(totals[c], axis=0, keepdims=True)
        cost = jnp.sum(totals[chunks + c], axis=0, keepdims=True) * (1.0 / SCALE)
        out_ref[2 * c] = jnp.where(low, plan, pltpu.roll(cost, share, 1))
        out_ref[2 * c + 1] = jnp.where(low, pltpu.roll(plan, share, 1), cost)


def own_half(ref, index):
    line = ref[pl.ds(lax.div(index, 2), 1)]
    share = LANES // 2
    moved = pltpu.roll(line, share, 1)
    return jnp.where(lax.rem(index, 2) == 0, line, moved)[:, :share]


def finish_kernel(log_cols, ratio, sums_ref, phi_ref, gamma_ref, phi_out, gamma_out, reward_out):
    total = sums_ref[0]
    for peer in range(1, sums_ref.shape[0]):
        total = total + sums_ref[peer]
    share = LANES // 2
    plan, cost = total[:, :share], pltpu.roll(total, share, 1)[:, :share]
    phi_out[...] = own_half(phi_ref, lax.axis_index("zh") * 4 + lax.axis_index("zl")) * LN2
    spot = lax.axis_index("core") * 16 + lax.axis_index("y") * 4 + lax.axis_index("x")
    gamma_out[...] = (own_half(gamma_ref, spot) - log_cols - jnp.log2(plan)) * LN2
    reward_out[...] = -ratio * cost / plan


def call(kernel, outs, scratch, *args):
    return pl.pallas_call(
        kernel,
        out_shape=outs,
        in_specs=[VMEM] * len(args),
        out_specs=jax.tree.map(lambda _: VMEM, outs),
        scratch_shapes=scratch,
        compiler_params=PARAMS,
    )(*args)


def body(demo, rollout):
    f32, bf16 = jnp.float32, jnp.bfloat16
    shape = jax.ShapeDtypeStruct
    share, width = demo.shape
    n_zh, n_line, n_sheet = lax.axis_size("zh"), lax.axis_size(LINE), lax.axis_size(SHEET)
    rows, cols = share * n_line, share * n_sheet
    log_rows, log_cols = math.log2(rows * n_sheet), math.log2(cols * n_line)
    row_vec, col_vec = (rows // LANES, LANES), (cols // LANES, LANES)
    tile = shape((cols // LANES, rows, LANES), f32)
    column = pltpu.VMEM((rows, LANES), f32)

    both = lax.optimization_barrier(jnp.concatenate([demo, rollout]))
    demo_send, rollout_send = call(
        prepare_kernel,
        (shape((share, width), bf16), shape((n_sheet, share, width), bf16)),
        [],
        both,
    )
    rollout_unit = lax.all_to_all(rollout_send, SHEET, 0, 0, tiled=True).reshape(cols, width)
    demo_unit = lax.all_gather(demo_send, ROW, axis_index_groups=TURNS, axis=0, tiled=True)

    inner, row_parts = call(
        row_lse_kernel,
        (tile, shape((n_line,) + row_vec, f32)),
        [column, column],
        demo_unit,
        rollout_unit,
    )
    row_parts = lax.all_to_all(row_parts, ROW, 0, 0, axis_index_groups=TURNS, tiled=True)
    phi, spread, col_parts = call(
        functools.partial(col_lse_kernel, log_rows),
        (shape(row_vec, f32), shape((rows, LANES), f32), shape((n_sheet,) + col_vec, f32)),
        [pltpu.VMEM(col_vec, f32)],
        row_parts,
        inner,
    )
    col_parts = lax.all_to_all(col_parts, SHEET, 0, 0, tiled=True)
    gamma, plan, row_parts = call(
        functools.partial(row_sum_kernel, log_cols),
        (shape(col_vec, f32), tile, shape((n_line,) + row_vec, f32)),
        [column],
        col_parts,
        spread,
        inner,
    )
    row_parts = lax.all_to_all(row_parts, ROW, 0, 0, axis_index_groups=TURNS, tiled=True)
    phi, sums = call(
        functools.partial(col_sum_kernel, log_rows),
        (shape(row_vec, f32), shape((n_sheet, 1, 2 * share), f32)),
        [column],
        row_parts,
        phi,
        plan,
        inner,
    )
    sums = lax.all_to_all(sums, SHEET, 0, 0, tiled=True)
    outs = call(
        functools.partial(finish_kernel, log_cols, 2.0 ** (log_cols - log_rows)),
        (shape((1, share), f32),) * 3,
        [],
        sums,
        phi,
        gamma,
    )
    return tuple(out.reshape(share) for out in outs)


def solution(mesh):
    fine = Mesh(mesh.devices.reshape(4, 4, 2, 4, 4), ALL)
    return jax.shard_map(
        body,
        mesh=fine,
        in_specs=(P(ALL, None), P(ALL, None)),
        out_specs=(P(ALL), P(ALL), P(ALL)),
        check_vma=False,
    )
```

```python
import functools
import math

import jax
import jax.numpy as jnp
from jax import lax
from jax.experimental import pallas as pl
from jax.experimental.pallas import tpu as pltpu
from jax.sharding import Mesh
from jax.sharding import PartitionSpec as P

EPS = 0.005
SCALE = 1.0 / (EPS * math.log(2.0))
LN2 = math.log(2.0)
LANES = 128
CHUNK = 256
PLANE = ("y", "x")
SHEET = ("y", "x", "zl")
LINE = ("zh", "core")
ALL = ("zh", "zl", "core", "y", "x")
VMEM = pl.BlockSpec(memory_space=pltpu.VMEM)
PARAMS = pltpu.CompilerParams(vmem_limit_bytes=6 * 1024 * 1024)


def normalize(embed):
    values = embed.astype(jnp.float32)
    inverse = lax.rsqrt(jnp.sum(values * values, axis=-1, keepdims=True) + 1e-06)
    return (values * inverse).astype(jnp.bfloat16)


def inner_of(left, right):
    return lax.dot_general(
        left, right, (((1,), (1,)), ((), ())), preferred_element_type=jnp.float32
    )


def log_total(parts):
    top = jnp.max(parts, axis=0)
    return top + jnp.log2(jnp.sum(jnp.exp2(parts - top[None]), axis=0))


def spread_rows(vector, column_ref):
    for block in range(vector.shape[0]):
        wide = jnp.broadcast_to(vector[block : block + 1], (LANES, LANES))
        column_ref[block * LANES : (block + 1) * LANES] = wide.T


def prepare_kernel(both_ref, demo_out, rollout_out):
    unit = normalize(both_ref[...])
    share = demo_out.shape[0]
    demo_out[...] = unit[:share]
    rollout_out[...] = unit[share:]


def copies_kernel(in_ref, out_ref):
    for peer in range(out_ref.shape[0]):
        out_ref[peer] = in_ref[...]


def row_lse_kernel(demo_ref, rollout_ref, inner_ref, out_ref, top_ref, total_ref):
    chunks, rows = inner_ref.shape[:2]
    for c in range(chunks // 2):
        inner = inner_of(demo_ref[...], rollout_ref[c * CHUNK : (c + 1) * CHUNK]) * SCALE
        left, right = inner[:, :LANES], inner[:, LANES:]
        inner_ref[2 * c] = left
        inner_ref[2 * c + 1] = right
        peak = jnp.maximum(left, right)
        top_ref[...] = peak if c == 0 else jnp.maximum(top_ref[...], peak)

    for row in range(0, rows, 64):
        at = slice(row, row + 64)
        top = top_ref[at]
        total = jnp.zeros_like(top)
        for c in range(chunks):
            total = total + jnp.exp2(inner_ref[c, at] - top)
        total_ref[at] = total
    for block in range(rows // LANES):
        at = slice(block * LANES, (block + 1) * LANES)
        top, total = top_ref[at].T, total_ref[at].T
        peak = jnp.max(top, axis=0, keepdims=True)
        total = jnp.sum(total * jnp.exp2(top - peak), axis=0, keepdims=True)
        line = peak - SCALE + jnp.log2(total)
        out_ref[:, block : block + 1] = jnp.broadcast_to(line[None], (out_ref.shape[0], 1, LANES))


def fold(op, values):
    while len(values) > 1:
        values = [op(*pair) for pair in zip(values[::2], values[1::2])]
    return values[0]


def col_lse_kernel(log_rows, parts_ref, inner_ref, phi_ref, column_ref, out_ref, line_ref):
    phi = -log_rows - log_total(parts_ref[...])
    phi_ref[...] = phi
    spread_rows(phi - SCALE, column_ref)
    chunks, rows = inner_ref.shape[:2]
    width, strip, strips = 4, 64, 4

    def group(g, _):
        def some_rows(b, carry):
            tops, totals = list(carry[:width]), list(carry[width:])
            for s in range(strips):
                expos = [[] for _ in range(width)]
                for row in range(0, strip, 8):
                    at = pl.ds(pl.multiple_of((b * strips + s) * strip + row, 8), 8)
                    column = column_ref[at]
                    for w in range(width):
                        expos[w].append(inner_ref[g * width + w, at] + column)
                for w in range(width):
                    top = jnp.maximum(tops[w], fold(jnp.maximum, expos[w]))
                    total = fold(jnp.add, [jnp.exp2(expo - top) for expo in expos[w]])
                    totals[w] = totals[w] * jnp.exp2(tops[w] - top) + total
                    tops[w] = top
            return tuple(tops + totals)

        zero = jnp.zeros((8, LANES), jnp.float32)
        carry = (zero - 1e30,) * width + (zero,) * width
        carry = lax.fori_loop(0, rows // (strip * strips), some_rows, carry)
        for w in range(width):
            peak = jnp.max(carry[w], axis=0, keepdims=True)
            total = carry[width + w] * jnp.exp2(carry[w] - peak)
            total = jnp.sum(total, axis=0, keepdims=True)
            line_ref[pl.ds(g * width + w, 1)] = peak + jnp.log2(total)
        return 0

    lax.fori_loop(0, chunks // width, group, 0)
    out_ref[...] = jnp.broadcast_to(line_ref[...][None], out_ref.shape)


def row_sum_kernel(
    log_cols, parts_ref, column_ref, inner_ref, gamma_ref, plan_ref, out_ref, total_ref
):
    gamma = -log_cols - log_total(parts_ref[...])
    gamma_ref[...] = gamma
    chunks, rows = inner_ref.shape[:2]
    for row in range(0, rows, LANES):
        at = slice(row, row + LANES)
        column = column_ref[at]
        total = jnp.zeros_like(column)
        for c in range(chunks):
            plan = jnp.exp2(inner_ref[c, at] + (column + gamma[c : c + 1]))
            plan_ref[c, at] = plan
            total = total + plan
        total_ref[at] = total
    for block in range(rows // LANES):
        total = total_ref[block * LANES : (block + 1) * LANES].T
        line = jnp.sum(total, axis=0, keepdims=True)
        out_ref[:, block : block + 1] = jnp.broadcast_to(line[None], (out_ref.shape[0], 1, LANES))


def col_sum_kernel(
    log_rows, parts_ref, phi_ref, plan_ref, inner_ref, phi_out, out_ref, column_ref
):
    change = -log_rows - jnp.log2(jnp.sum(parts_ref[...], axis=0))
    phi_out[...] = phi_ref[...] + change
    spread_rows(jnp.exp2(change), column_ref)
    chunks, rows = plan_ref.shape[:2]
    step = 128

    def add_up(b, totals):
        totals = list(totals)
        for row in range(0, step, 8):
            at = pl.ds(pl.multiple_of(b * step + row, 8), 8)
            column = column_ref[at]
            for c in range(chunks):
                plan = plan_ref[c, at] * column
                totals[c] = totals[c] + plan
                totals[chunks + c] = totals[chunks + c] + plan * (SCALE - inner_ref[c, at])
        return tuple(totals)

    zero = jnp.zeros((8, LANES), jnp.float32)
    totals = lax.fori_loop(0, rows // step, add_up, (zero,) * (2 * chunks), unroll=2)
    share = LANES // 2
    low = lax.broadcasted_iota(jnp.int32, (1, LANES), 1) < share
    for c in range(chunks):
        plan = jnp.sum(totals[c], axis=0, keepdims=True)
        cost = jnp.sum(totals[chunks + c], axis=0, keepdims=True) * (1.0 / SCALE)
        out_ref[2 * c] = jnp.where(low, plan, pltpu.roll(cost, share, 1))
        out_ref[2 * c + 1] = jnp.where(low, pltpu.roll(plan, share, 1), cost)


def own_half(ref, index):
    line = ref[pl.ds(lax.div(index, 2), 1)]
    share = LANES // 2
    moved = pltpu.roll(line, share, 1)
    return jnp.where(lax.rem(index, 2) == 0, line, moved)[:, :share]


def finish_kernel(log_cols, ratio, sums_ref, phi_ref, gamma_ref, phi_out, gamma_out, reward_out):
    total = sums_ref[0]
    for peer in range(1, sums_ref.shape[0]):
        total = total + sums_ref[peer]
    share = LANES // 2
    plan, cost = total[:, :share], pltpu.roll(total, share, 1)[:, :share]
    phi_out[...] = own_half(phi_ref, lax.axis_index("zh") * 2 + lax.axis_index("core")) * LN2
    spot = lax.axis_index("y") * 8 + lax.axis_index("x") * 2 + lax.axis_index("zl")
    gamma_out[...] = (own_half(gamma_ref, spot) - log_cols - jnp.log2(plan)) * LN2
    reward_out[...] = -ratio * cost / plan


def call(kernel, outs, scratch, *args):
    return pl.pallas_call(
        kernel,
        out_shape=outs,
        in_specs=[VMEM] * len(args),
        out_specs=jax.tree.map(lambda _: VMEM, outs),
        scratch_shapes=scratch,
        compiler_params=PARAMS,
    )(*args)


def body(demo, rollout):
    f32, bf16 = jnp.float32, jnp.bfloat16
    shape = jax.ShapeDtypeStruct
    share, width = demo.shape
    n_plane = lax.axis_size(PLANE)
    n_line, n_sheet = lax.axis_size(LINE), lax.axis_size(SHEET)
    rows, cols = share * n_line, share * n_sheet
    log_rows, log_cols = math.log2(rows * n_sheet), math.log2(cols * n_line)
    row_vec, col_vec = (rows // LANES, LANES), (cols // LANES, LANES)
    tile = shape((cols // LANES, rows, LANES), f32)
    column = pltpu.VMEM((rows, LANES), f32)

    both = lax.optimization_barrier(jnp.concatenate([demo, rollout]))
    own = shape((share, width), bf16)
    demo_send, rollout_send = call(prepare_kernel, (own, own), [], both)
    pair = lax.all_gather(rollout_send, "zl", axis=0, tiled=True)
    pairs = call(copies_kernel, shape((n_plane, 2 * share, width), bf16), [], pair)
    rollout_unit = lax.all_to_all(pairs, PLANE, 0, 0, tiled=True).reshape(cols, width)
    demo_unit = lax.all_gather(demo_send, LINE, axis=0, tiled=True)

    inner, row_parts = call(
        row_lse_kernel,
        (tile, shape((n_line,) + row_vec, f32)),
        [column, column],
        demo_unit,
        rollout_unit,
    )
    row_parts = lax.all_to_all(row_parts, LINE, 0, 0, tiled=True)
    phi, spread, col_parts = call(
        functools.partial(col_lse_kernel, log_rows),
        (shape(row_vec, f32), shape((rows, LANES), f32), shape((n_sheet,) + col_vec, f32)),
        [pltpu.VMEM(col_vec, f32)],
        row_parts,
        inner,
    )
    col_parts = lax.all_to_all(col_parts, SHEET, 0, 0, tiled=True)
    gamma, plan, row_parts = call(
        functools.partial(row_sum_kernel, log_cols),
        (shape(col_vec, f32), tile, shape((n_line,) + row_vec, f32)),
        [column],
        col_parts,
        spread,
        inner,
    )
    row_parts = lax.all_to_all(row_parts, LINE, 0, 0, tiled=True)
    phi, sums = call(
        functools.partial(col_sum_kernel, log_rows),
        (shape(row_vec, f32), shape((n_sheet, 1, 2 * share), f32)),
        [column],
        row_parts,
        phi,
        plan,
        inner,
    )
    sums = lax.all_to_all(sums, SHEET, 0, 0, tiled=True)
    outs = call(
        functools.partial(finish_kernel, log_cols, 2.0 ** (log_cols - log_rows)),
        (shape((1, share), f32),) * 3,
        [],
        sums,
        phi,
        gamma,
    )
    return tuple(out.reshape(share) for out in outs)


def solution(mesh):
    fine = Mesh(mesh.devices.reshape(8, 2, 2, 4, 4), ALL)
    return jax.shard_map(
        body,
        mesh=fine,
        in_specs=(P(ALL, None), P(ALL, None)),
        out_specs=(P(ALL), P(ALL), P(ALL)),
        check_vma=False,
    )
```

```python
import functools
import math

import jax
import jax.numpy as jnp
from jax import lax
from jax.experimental import pallas as pl
from jax.experimental.pallas import tpu as pltpu
from jax.sharding import Mesh
from jax.sharding import PartitionSpec as P

EPS = 0.005
SCALE = 1.0 / (EPS * math.log(2.0))
LN2 = math.log(2.0)
LANES = 128
CHUNK = 256
PLANE = ("y", "x")
SHEET = ("y", "x", "zl")
LINE = ("zh", "core")
ALL = ("zh", "zl", "core", "y", "x")
VMEM = pl.BlockSpec(memory_space=pltpu.VMEM)
PARAMS = pltpu.CompilerParams(vmem_limit_bytes=6 * 1024 * 1024)


def normalize(embed):
    values = embed.astype(jnp.float32)
    inverse = lax.rsqrt(jnp.sum(values * values, axis=-1, keepdims=True) + 1e-06)
    return (values * inverse).astype(jnp.bfloat16)


def inner_of(left, right):
    return lax.dot_general(
        left, right, (((1,), (1,)), ((), ())), preferred_element_type=jnp.float32
    )


def log_total(parts):
    top = jnp.max(parts, axis=0)
    return top + jnp.log2(jnp.sum(jnp.exp2(parts - top[None]), axis=0))


def spread_rows(vector, column_ref):
    for block in range(vector.shape[0]):
        wide = jnp.broadcast_to(vector[block : block + 1], (LANES, LANES))
        column_ref[block * LANES : (block + 1) * LANES] = wide.T


def prepare_kernel(both_ref, demo_out, rollout_out):
    unit = normalize(both_ref[...])
    share = demo_out.shape[0]
    demo_out[...] = unit[:share]
    rollout_out[...] = unit[share:]


def copies_kernel(in_ref, out_ref):
    for peer in range(out_ref.shape[0]):
        out_ref[peer] = in_ref[...]


def row_lse_kernel(demo_ref, rollout_ref, inner_ref, out_ref, top_ref, total_ref):
    chunks, rows = inner_ref.shape[:2]
    for c in range(chunks // 2):
        inner = inner_of(demo_ref[...], rollout_ref[c * CHUNK : (c + 1) * CHUNK]) * SCALE
        left, right = inner[:, :LANES], inner[:, LANES:]
        inner_ref[2 * c] = left
        inner_ref[2 * c + 1] = right
        peak = jnp.maximum(left, right)
        top_ref[...] = peak if c == 0 else jnp.maximum(top_ref[...], peak)

    for row in range(0, rows, 64):
        at = slice(row, row + 64)
        top = top_ref[at]
        total = jnp.zeros_like(top)
        for c in range(chunks):
            total = total + jnp.exp2(inner_ref[c, at] - top)
        total_ref[at] = total
    for block in range(rows // LANES):
        at = slice(block * LANES, (block + 1) * LANES)
        top, total = top_ref[at].T, total_ref[at].T
        peak = jnp.max(top, axis=0, keepdims=True)
        total = jnp.sum(total * jnp.exp2(top - peak), axis=0, keepdims=True)
        line = peak - SCALE + jnp.log2(total)
        out_ref[:, block : block + 1] = jnp.broadcast_to(line[None], (out_ref.shape[0], 1, LANES))


def fold(op, values):
    while len(values) > 1:
        values = [op(*pair) for pair in zip(values[::2], values[1::2])]
    return values[0]


def col_lse_kernel(log_rows, parts_ref, inner_ref, phi_ref, column_ref, out_ref, line_ref):
    phi = -log_rows - log_total(parts_ref[...])
    phi_ref[...] = phi
    spread_rows(phi - SCALE, column_ref)
    chunks, rows = inner_ref.shape[:2]
    width, strip, strips = 4, 64, 4

    def group(g, _):
        def some_rows(b, carry):
            tops, totals = list(carry[:width]), list(carry[width:])
            for s in range(strips):
                expos = [[] for _ in range(width)]
                for row in range(0, strip, 8):
                    at = pl.ds(pl.multiple_of((b * strips + s) * strip + row, 8), 8)
                    column = column_ref[at]
                    for w in range(width):
                        expos[w].append(inner_ref[g * width + w, at] + column)
                for w in range(width):
                    top = jnp.maximum(tops[w], fold(jnp.maximum, expos[w]))
                    total = fold(jnp.add, [jnp.exp2(expo - top) for expo in expos[w]])
                    totals[w] = totals[w] * jnp.exp2(tops[w] - top) + total
                    tops[w] = top
            return tuple(tops + totals)

        zero = jnp.zeros((8, LANES), jnp.float32)
        carry = (zero - 1e30,) * width + (zero,) * width
        carry = lax.fori_loop(0, rows // (strip * strips), some_rows, carry)
        for w in range(width):
            peak = jnp.max(carry[w], axis=0, keepdims=True)
            total = carry[width + w] * jnp.exp2(carry[w] - peak)
            total = jnp.sum(total, axis=0, keepdims=True)
            line_ref[pl.ds(g * width + w, 1)] = peak + jnp.log2(total)
        return 0

    lax.fori_loop(0, chunks // width, group, 0)
    out_ref[...] = jnp.broadcast_to(line_ref[...][None], out_ref.shape)


def row_sum_kernel(
    log_cols, parts_ref, column_ref, inner_ref, gamma_ref, plan_ref, out_ref, total_ref
):
    gamma = -log_cols - log_total(parts_ref[...])
    gamma_ref[...] = gamma
    chunks, rows = inner_ref.shape[:2]
    for row in range(0, rows, LANES):
        at = slice(row, row + LANES)
        column = column_ref[at]
        total = jnp.zeros_like(column)
        for c in range(chunks):
            plan = jnp.exp2(inner_ref[c, at] + (column + gamma[c : c + 1]))
            plan_ref[c, at] = plan
            total = total + plan
        total_ref[at] = total
    lines = []
    for block in range(rows // LANES):
        total = total_ref[block * LANES : (block + 1) * LANES].T
        lines.append(jnp.sum(total, axis=0, keepdims=True))
    peers = out_ref.shape[0] // len(lines)
    out_ref[...] = jnp.concatenate(lines * peers).astype(out_ref.dtype)


def col_sum_kernel(
    log_rows, parts_ref, phi_ref, plan_ref, inner_ref, phi_out, out_ref, column_ref
):
    blocks = phi_ref.shape[0]
    parts = parts_ref[...].astype(jnp.float32)
    total = parts[:blocks]
    for peer in range(1, parts.shape[0] // blocks):
        total = total + parts[peer * blocks : (peer + 1) * blocks]
    change = -log_rows - jnp.log2(total)
    phi_out[...] = phi_ref[...] + change
    spread_rows(jnp.exp2(change), column_ref)
    chunks, rows = plan_ref.shape[:2]
    step = 128

    def add_up(b, totals):
        totals = list(totals)
        for row in range(0, step, 8):
            at = pl.ds(pl.multiple_of(b * step + row, 8), 8)
            column = column_ref[at]
            for c in range(chunks):
                plan = plan_ref[c, at] * column
                totals[c] = totals[c] + plan
                totals[chunks + c] = totals[chunks + c] + plan * (SCALE - inner_ref[c, at])
        return tuple(totals)

    zero = jnp.zeros((8, LANES), jnp.float32)
    totals = lax.fori_loop(0, rows // step, add_up, (zero,) * (2 * chunks), unroll=2)
    share = LANES // 2
    low = lax.broadcasted_iota(jnp.int32, (1, LANES), 1) < share
    for c in range(chunks):
        plan = jnp.sum(totals[c], axis=0, keepdims=True)
        cost = jnp.sum(totals[chunks + c], axis=0, keepdims=True) * (1.0 / SCALE)
        out_ref[2 * c] = jnp.where(low, plan, pltpu.roll(cost, share, 1))
        out_ref[2 * c + 1] = jnp.where(low, pltpu.roll(plan, share, 1), cost)


def own_half(ref, index):
    line = ref[pl.ds(lax.div(index, 2), 1)]
    share = LANES // 2
    moved = pltpu.roll(line, share, 1)
    return jnp.where(lax.rem(index, 2) == 0, line, moved)[:, :share]


def finish_kernel(log_cols, ratio, sums_ref, phi_ref, gamma_ref, phi_out, gamma_out, reward_out):
    total = sums_ref[0]
    for peer in range(1, sums_ref.shape[0]):
        total = total + sums_ref[peer]
    share = LANES // 2
    plan, cost = total[:, :share], pltpu.roll(total, share, 1)[:, :share]
    phi_out[...] = own_half(phi_ref, lax.axis_index("zh") * 2 + lax.axis_index("core")) * LN2
    spot = lax.axis_index("y") * 8 + lax.axis_index("x") * 2 + lax.axis_index("zl")
    gamma_out[...] = (own_half(gamma_ref, spot) - log_cols - jnp.log2(plan)) * LN2
    reward_out[...] = -ratio * cost / plan


def call(kernel, outs, scratch, *args):
    return pl.pallas_call(
        kernel,
        out_shape=outs,
        in_specs=[VMEM] * len(args),
        out_specs=jax.tree.map(lambda _: VMEM, outs),
        scratch_shapes=scratch,
        compiler_params=PARAMS,
    )(*args)


def body(demo, rollout):
    f32, bf16 = jnp.float32, jnp.bfloat16
    shape = jax.ShapeDtypeStruct
    share, width = demo.shape
    n_plane = lax.axis_size(PLANE)
    n_line, n_sheet = lax.axis_size(LINE), lax.axis_size(SHEET)
    rows, cols = share * n_line, share * n_sheet
    log_rows, log_cols = math.log2(rows * n_sheet), math.log2(cols * n_line)
    row_vec, col_vec = (rows // LANES, LANES), (cols // LANES, LANES)
    tile = shape((cols // LANES, rows, LANES), f32)
    column = pltpu.VMEM((rows, LANES), f32)

    both = lax.optimization_barrier(jnp.concatenate([demo, rollout]))
    own = shape((share, width), bf16)
    demo_send, rollout_send = call(prepare_kernel, (own, own), [], both)
    pair = lax.all_gather(rollout_send, "zl", axis=0, tiled=True)
    pairs = call(copies_kernel, shape((n_plane, 2 * share, width), bf16), [], pair)
    rollout_unit = lax.all_to_all(pairs, PLANE, 0, 0, tiled=True).reshape(cols, width)
    demo_unit = lax.all_gather(demo_send, LINE, axis=0, tiled=True)

    inner, row_parts = call(
        row_lse_kernel,
        (tile, shape((n_line,) + row_vec, f32)),
        [column, column],
        demo_unit,
        rollout_unit,
    )
    row_parts = lax.all_to_all(row_parts, LINE, 0, 0, tiled=True)
    phi, spread, col_parts = call(
        functools.partial(col_lse_kernel, log_rows),
        (shape(row_vec, f32), shape((rows, LANES), f32), shape((n_sheet,) + col_vec, f32)),
        [pltpu.VMEM(col_vec, f32)],
        row_parts,
        inner,
    )
    col_parts = lax.all_to_all(col_parts, SHEET, 0, 0, tiled=True)
    gamma, plan, row_parts = call(
        functools.partial(row_sum_kernel, log_cols),
        (shape(col_vec, f32), tile, shape((n_line * row_vec[0], LANES), bf16)),
        [column],
        col_parts,
        spread,
        inner,
    )
    row_parts = row_parts.reshape((n_line,) + row_vec)
    row_parts = lax.all_to_all(row_parts, LINE, 0, 0, tiled=True)
    row_parts = row_parts.reshape(n_line * row_vec[0], LANES)
    phi, sums = call(
        functools.partial(col_sum_kernel, log_rows),
        (shape(row_vec, f32), shape((n_sheet, 1, 2 * share), f32)),
        [column],
        row_parts,
        phi,
        plan,
        inner,
    )
    sums = lax.all_to_all(sums, SHEET, 0, 0, tiled=True)
    outs = call(
        functools.partial(finish_kernel, log_cols, 2.0 ** (log_cols - log_rows)),
        (shape((1, share), f32),) * 3,
        [],
        sums,
        phi,
        gamma,
    )
    return tuple(out.reshape(share) for out in outs)


def solution(mesh):
    fine = Mesh(mesh.devices.reshape(8, 2, 2, 4, 4), ALL)
    return jax.shard_map(
        body,
        mesh=fine,
        in_specs=(P(ALL, None), P(ALL, None)),
        out_specs=(P(ALL), P(ALL), P(ALL)),
        check_vma=False,
    )
```

```python
import functools
import math

import jax
import jax.numpy as jnp
from jax import lax
from jax.experimental import pallas as pl
from jax.experimental.pallas import tpu as pltpu
from jax.sharding import Mesh
from jax.sharding import PartitionSpec as P

EPS = 0.005
SCALE = 1.0 / (EPS * math.log(2.0))
LN2 = math.log(2.0)
LANES = 128
CHUNK = 256
PLANE = ("y", "x")
SHEET = ("y", "x", "zl")
LINE = ("zh", "core")
ALL = ("zh", "zl", "core", "y", "x")
VMEM = pl.BlockSpec(memory_space=pltpu.VMEM)
PARAMS = pltpu.CompilerParams(vmem_limit_bytes=6 * 1024 * 1024)


def normalize(embed):
    values = embed.astype(jnp.float32)
    inverse = lax.rsqrt(jnp.sum(values * values, axis=-1, keepdims=True) + 1e-06)
    return (values * inverse).astype(jnp.bfloat16)


def inner_of(left, right):
    return lax.dot_general(
        left, right, (((1,), (1,)), ((), ())), preferred_element_type=jnp.float32
    )


def log_total(parts):
    top = jnp.max(parts, axis=0)
    return top + jnp.log2(jnp.sum(jnp.exp2(parts - top[None]), axis=0))


def spread_rows(vector, column_ref):
    for block in range(vector.shape[0]):
        wide = jnp.broadcast_to(vector[block : block + 1], (LANES, LANES))
        column_ref[block * LANES : (block + 1) * LANES] = wide.T


def prepare_kernel(pair_ref, pair_out):
    pair = normalize(pair_ref[...])
    for peer in range(pair_out.shape[0]):
        pair_out[peer] = pair


def row_lse_kernel(
    raw_ref, rollout_ref, inner_ref, out_ref, demo_ref, top_ref, total_ref
):
    chunks, rows = inner_ref.shape[:2]
    for row in range(0, rows, LANES):
        demo_ref[row : row + LANES] = normalize(raw_ref[row : row + LANES])
    for c in range(chunks // 2):
        inner = inner_of(demo_ref[...], rollout_ref[c * CHUNK : (c + 1) * CHUNK]) * SCALE
        left, right = inner[:, :LANES], inner[:, LANES:]
        inner_ref[2 * c] = left
        inner_ref[2 * c + 1] = right
        peak = jnp.maximum(left, right)
        top_ref[...] = peak if c == 0 else jnp.maximum(top_ref[...], peak)

    for row in range(0, rows, 64):
        at = slice(row, row + 64)
        top = top_ref[at]
        total = jnp.zeros_like(top)
        for c in range(chunks):
            total = total + jnp.exp2(inner_ref[c, at] - top)
        total_ref[at] = total
    for block in range(rows // LANES):
        at = slice(block * LANES, (block + 1) * LANES)
        top, total = top_ref[at].T, total_ref[at].T
        peak = jnp.max(top, axis=0, keepdims=True)
        total = jnp.sum(total * jnp.exp2(top - peak), axis=0, keepdims=True)
        line = peak - SCALE + jnp.log2(total)
        out_ref[:, block : block + 1] = jnp.broadcast_to(line[None], (out_ref.shape[0], 1, LANES))


def fold(op, values):
    while len(values) > 1:
        values = [op(*pair) for pair in zip(values[::2], values[1::2])]
    return values[0]


def col_lse_kernel(log_rows, parts_ref, inner_ref, phi_ref, column_ref, out_ref, line_ref):
    phi = -log_rows - log_total(parts_ref[...])
    phi_ref[...] = phi
    spread_rows(phi - SCALE, column_ref)
    chunks, rows = inner_ref.shape[:2]
    width, strip, strips = 4, 64, 4

    def group(g, _):
        def some_rows(b, carry):
            tops, totals = list(carry[:width]), list(carry[width:])
            for s in range(strips):
                expos = [[] for _ in range(width)]
                for row in range(0, strip, 8):
                    at = pl.ds(pl.multiple_of((b * strips + s) * strip + row, 8), 8)
                    column = column_ref[at]
                    for w in range(width):
                        expos[w].append(inner_ref[g * width + w, at] + column)
                for w in range(width):
                    top = jnp.maximum(tops[w], fold(jnp.maximum, expos[w]))
                    total = fold(jnp.add, [jnp.exp2(expo - top) for expo in expos[w]])
                    totals[w] = totals[w] * jnp.exp2(tops[w] - top) + total
                    tops[w] = top
            return tuple(tops + totals)

        zero = jnp.zeros((8, LANES), jnp.float32)
        carry = (zero - 1e30,) * width + (zero,) * width
        carry = lax.fori_loop(0, rows // (strip * strips), some_rows, carry)
        for w in range(width):
            peak = jnp.max(carry[w], axis=0, keepdims=True)
            total = carry[width + w] * jnp.exp2(carry[w] - peak)
            total = jnp.sum(total, axis=0, keepdims=True)
            line_ref[pl.ds(g * width + w, 1)] = peak + jnp.log2(total)
        return 0

    lax.fori_loop(0, chunks // width, group, 0)
    out_ref[...] = jnp.broadcast_to(line_ref[...][None], out_ref.shape)


def row_sum_kernel(
    log_cols, parts_ref, column_ref, inner_ref, gamma_ref, plan_ref, out_ref, total_ref
):
    gamma = -log_cols - log_total(parts_ref[...])
    gamma_ref[...] = gamma
    chunks, rows = inner_ref.shape[:2]
    for row in range(0, rows, LANES):
        at = slice(row, row + LANES)
        column = column_ref[at]
        total = jnp.zeros_like(column)
        for c in range(chunks):
            plan = jnp.exp2(inner_ref[c, at] + (column + gamma[c : c + 1]))
            plan_ref[c, at] = plan
            total = total + plan
        total_ref[at] = total
    lines = []
    for block in range(rows // LANES):
        total = total_ref[block * LANES : (block + 1) * LANES].T
        lines.append(jnp.sum(total, axis=0, keepdims=True))
    peers = out_ref.shape[0] // len(lines)
    out_ref[...] = jnp.concatenate(lines * peers).astype(out_ref.dtype)


def col_sum_kernel(
    log_rows, parts_ref, phi_ref, plan_ref, inner_ref, phi_out, out_ref, column_ref
):
    blocks = phi_ref.shape[0]
    parts = parts_ref[...].astype(jnp.float32)
    total = parts[:blocks]
    for peer in range(1, parts.shape[0] // blocks):
        total = total + parts[peer * blocks : (peer + 1) * blocks]
    change = -log_rows - jnp.log2(total)
    phi_out[...] = phi_ref[...] + change
    spread_rows(jnp.exp2(change), column_ref)
    chunks, rows = plan_ref.shape[:2]
    step = 128

    def add_up(b, totals):
        totals = list(totals)
        for row in range(0, step, 8):
            at = pl.ds(pl.multiple_of(b * step + row, 8), 8)
            column = column_ref[at]
            for c in range(chunks):
                plan = plan_ref[c, at] * column
                totals[c] = totals[c] + plan
                totals[chunks + c] = totals[chunks + c] + plan * (SCALE - inner_ref[c, at])
        return tuple(totals)

    zero = jnp.zeros((8, LANES), jnp.float32)
    totals = lax.fori_loop(0, rows // step, add_up, (zero,) * (2 * chunks), unroll=2)
    share = LANES // 2
    low = lax.broadcasted_iota(jnp.int32, (1, LANES), 1) < share
    for c in range(chunks):
        plan = jnp.sum(totals[c], axis=0, keepdims=True)
        cost = jnp.sum(totals[chunks + c], axis=0, keepdims=True) * (1.0 / SCALE)
        out_ref[2 * c] = jnp.where(low, plan, pltpu.roll(cost, share, 1))
        out_ref[2 * c + 1] = jnp.where(low, pltpu.roll(plan, share, 1), cost)


def own_half(ref, index):
    line = ref[pl.ds(lax.div(index, 2), 1)]
    share = LANES // 2
    moved = pltpu.roll(line, share, 1)
    return jnp.where(lax.rem(index, 2) == 0, line, moved)[:, :share]


def finish_kernel(log_cols, ratio, sums_ref, phi_ref, gamma_ref, phi_out, gamma_out, reward_out):
    total = sums_ref[0]
    for peer in range(1, sums_ref.shape[0]):
        total = total + sums_ref[peer]
    share = LANES // 2
    plan, cost = total[:, :share], pltpu.roll(total, share, 1)[:, :share]
    phi_out[...] = own_half(phi_ref, lax.axis_index("zh") * 2 + lax.axis_index("core")) * LN2
    spot = lax.axis_index("y") * 8 + lax.axis_index("x") * 2 + lax.axis_index("zl")
    gamma_out[...] = (own_half(gamma_ref, spot) - log_cols - jnp.log2(plan)) * LN2
    reward_out[...] = -ratio * cost / plan


def call(kernel, outs, scratch, *args):
    return pl.pallas_call(
        kernel,
        out_shape=outs,
        in_specs=[VMEM] * len(args),
        out_specs=jax.tree.map(lambda _: VMEM, outs),
        scratch_shapes=scratch,
        compiler_params=PARAMS,
    )(*args)


def body(demo, rollout):
    f32, bf16 = jnp.float32, jnp.bfloat16
    shape = jax.ShapeDtypeStruct
    share, width = demo.shape
    n_plane = lax.axis_size(PLANE)
    n_line, n_sheet = lax.axis_size(LINE), lax.axis_size(SHEET)
    rows, cols = share * n_line, share * n_sheet
    log_rows, log_cols = math.log2(rows * n_sheet), math.log2(cols * n_line)
    row_vec, col_vec = (rows // LANES, LANES), (cols // LANES, LANES)
    tile = shape((cols // LANES, rows, LANES), f32)
    column = pltpu.VMEM((rows, LANES), f32)

    pair = lax.all_gather(rollout, "zl", axis=0, tiled=True)
    pairs = call(prepare_kernel, shape((n_plane, 2 * share, width), bf16), [], pair)
    rollout_unit = lax.all_to_all(pairs, PLANE, 0, 0, tiled=True).reshape(cols, width)
    demo_unit = lax.all_gather(demo, LINE, axis=0, tiled=True)

    inner, row_parts = call(
        row_lse_kernel,
        (tile, shape((n_line,) + row_vec, f32)),
        [pltpu.VMEM((rows, width), bf16), column, column],
        demo_unit,
        rollout_unit,
    )
    row_parts = lax.all_to_all(row_parts, LINE, 0, 0, tiled=True)
    phi, spread, col_parts = call(
        functools.partial(col_lse_kernel, log_rows),
        (shape(row_vec, f32), shape((rows, LANES), f32), shape((n_sheet,) + col_vec, f32)),
        [pltpu.VMEM(col_vec, f32)],
        row_parts,
        inner,
    )
    col_parts = lax.all_to_all(col_parts, SHEET, 0, 0, tiled=True)
    gamma, plan, row_parts = call(
        functools.partial(row_sum_kernel, log_cols),
        (shape(col_vec, f32), tile, shape((n_line * row_vec[0], LANES), bf16)),
        [column],
        col_parts,
        spread,
        inner,
    )
    row_parts = row_parts.reshape((n_line,) + row_vec)
    row_parts = lax.all_to_all(row_parts, LINE, 0, 0, tiled=True)
    row_parts = row_parts.reshape(n_line * row_vec[0], LANES)
    phi, sums = call(
        functools.partial(col_sum_kernel, log_rows),
        (shape(row_vec, f32), shape((n_sheet, 1, 2 * share), f32)),
        [column],
        row_parts,
        phi,
        plan,
        inner,
    )
    sums = lax.all_to_all(sums, SHEET, 0, 0, tiled=True)
    outs = call(
        functools.partial(finish_kernel, log_cols, 2.0 ** (log_cols - log_rows)),
        (shape((1, share), f32),) * 3,
        [],
        sums,
        phi,
        gamma,
    )
    return tuple(out.reshape(share) for out in outs)


def solution(mesh):
    fine = Mesh(mesh.devices.reshape(8, 2, 2, 4, 4), ALL)
    return jax.shard_map(
        body,
        mesh=fine,
        in_specs=(P(ALL, None), P(ALL, None)),
        out_specs=(P(ALL), P(ALL), P(ALL)),
        check_vma=False,
    )
```

```python
import functools
import math

import jax
import jax.numpy as jnp
from jax import lax
from jax.experimental import pallas as pl
from jax.experimental.pallas import tpu as pltpu
from jax.sharding import Mesh
from jax.sharding import PartitionSpec as P

EPS = 0.005
SCALE = 1.0 / (EPS * math.log(2.0))
LN2 = math.log(2.0)
LANES = 128
CHUNK = 256
PLANE = ("y", "x")
SHEET = ("y", "x", "zl")
LINE = ("zh", "core")
ALL = ("zh", "zl", "core", "y", "x")
VMEM = pl.BlockSpec(memory_space=pltpu.VMEM)
PARAMS = pltpu.CompilerParams(vmem_limit_bytes=6 * 1024 * 1024)


def normalize(embed):
    values = embed.astype(jnp.float32)
    inverse = lax.rsqrt(jnp.sum(values * values, axis=-1, keepdims=True) + 1e-06)
    return (values * inverse).astype(jnp.bfloat16)


def inner_of(left, right):
    return lax.dot_general(
        left, right, (((1,), (1,)), ((), ())), preferred_element_type=jnp.float32
    )


def log_total(parts):
    top = jnp.max(parts, axis=0)
    return top + jnp.log2(jnp.sum(jnp.exp2(parts - top[None]), axis=0))


def lanes(chunk):
    return slice(chunk * LANES, (chunk + 1) * LANES)


def spread_rows(vector, column_ref):
    for block in range(vector.shape[0]):
        wide = jnp.broadcast_to(vector[block : block + 1], (LANES, LANES))
        column_ref[block * LANES : (block + 1) * LANES] = wide.T


def prepare_kernel(pair_ref, pair_out):
    pair = normalize(pair_ref[...])
    for peer in range(pair_out.shape[0]):
        pair_out[peer] = pair


def row_lse_kernel(
    raw_ref, rollout_ref, inner_ref, out_ref, demo_ref, top_ref, total_ref
):
    rows, chunks = inner_ref.shape[0], inner_ref.shape[1] // LANES
    for row in range(0, rows, LANES):
        demo_ref[row : row + LANES] = normalize(raw_ref[row : row + LANES])
    for c in range(chunks // 2):
        inner = inner_of(demo_ref[...], rollout_ref[c * CHUNK : (c + 1) * CHUNK]) * SCALE
        inner_ref[:, c * CHUNK : (c + 1) * CHUNK] = inner
        peak = jnp.maximum(inner[:, :LANES], inner[:, LANES:])
        top_ref[...] = peak if c == 0 else jnp.maximum(top_ref[...], peak)

    for row in range(0, rows, 64):
        at = slice(row, row + 64)
        top = top_ref[at]
        total = jnp.zeros_like(top)
        for c in range(chunks):
            total = total + jnp.exp2(inner_ref[at, lanes(c)] - top)
        total_ref[at] = total
    for block in range(rows // LANES):
        at = slice(block * LANES, (block + 1) * LANES)
        top, total = top_ref[at].T, total_ref[at].T
        peak = jnp.max(top, axis=0, keepdims=True)
        total = jnp.sum(total * jnp.exp2(top - peak), axis=0, keepdims=True)
        line = peak - SCALE + jnp.log2(total)
        out_ref[:, block : block + 1] = jnp.broadcast_to(line[None], (out_ref.shape[0], 1, LANES))


def fold(op, values):
    while len(values) > 1:
        values = [op(*pair) for pair in zip(values[::2], values[1::2])]
    return values[0]


def col_lse_kernel(log_rows, parts_ref, inner_ref, phi_ref, column_ref, out_ref, line_ref):
    phi = -log_rows - log_total(parts_ref[...])
    phi_ref[...] = phi
    spread_rows(phi - SCALE, column_ref)
    rows, chunks = inner_ref.shape[0], inner_ref.shape[1] // LANES
    width, strip, strips = 4, 64, 4

    for g in range(chunks // width):

        def some_rows(b, carry, g=g):
            tops, totals = list(carry[:width]), list(carry[width:])
            for s in range(strips):
                expos = [[] for _ in range(width)]
                for row in range(0, strip, 8):
                    at = pl.ds(pl.multiple_of((b * strips + s) * strip + row, 8), 8)
                    column = column_ref[at]
                    for w in range(width):
                        expos[w].append(inner_ref[at, lanes(g * width + w)] + column)
                for w in range(width):
                    top = jnp.maximum(tops[w], fold(jnp.maximum, expos[w]))
                    total = fold(jnp.add, [jnp.exp2(expo - top) for expo in expos[w]])
                    totals[w] = totals[w] * jnp.exp2(tops[w] - top) + total
                    tops[w] = top
            return tuple(tops + totals)

        zero = jnp.zeros((8, LANES), jnp.float32)
        carry = (zero - 1e30,) * width + (zero,) * width
        carry = lax.fori_loop(0, rows // (strip * strips), some_rows, carry, unroll=4)
        for w in range(width):
            peak = jnp.max(carry[w], axis=0, keepdims=True)
            total = carry[width + w] * jnp.exp2(carry[w] - peak)
            total = jnp.sum(total, axis=0, keepdims=True)
            line_ref[g * width + w : g * width + w + 1] = peak + jnp.log2(total)
    out_ref[...] = jnp.broadcast_to(line_ref[...][None], out_ref.shape)


def row_sum_kernel(
    log_cols, parts_ref, column_ref, inner_ref, gamma_ref, plan_ref, out_ref, total_ref
):
    gamma = -log_cols - log_total(parts_ref[...])
    gamma_ref[...] = gamma
    rows, chunks = inner_ref.shape[0], inner_ref.shape[1] // LANES
    for row in range(0, rows, LANES):
        at = slice(row, row + LANES)
        column = column_ref[at]
        total = jnp.zeros_like(column)
        for c in range(chunks):
            plan = jnp.exp2(inner_ref[at, lanes(c)] + (column + gamma[c : c + 1]))
            plan_ref[at, lanes(c)] = plan
            total = total + plan
        total_ref[at] = total
    lines = []
    for block in range(rows // LANES):
        total = total_ref[block * LANES : (block + 1) * LANES].T
        lines.append(jnp.sum(total, axis=0, keepdims=True))
    peers = out_ref.shape[0] // len(lines)
    out_ref[...] = jnp.concatenate(lines * peers).astype(out_ref.dtype)


def col_sum_kernel(
    log_rows, parts_ref, phi_ref, plan_ref, inner_ref, phi_out, out_ref, column_ref
):
    blocks = phi_ref.shape[0]
    parts = parts_ref[...].astype(jnp.float32)
    total = parts[:blocks]
    for peer in range(1, parts.shape[0] // blocks):
        total = total + parts[peer * blocks : (peer + 1) * blocks]
    change = -log_rows - jnp.log2(total)
    phi_out[...] = phi_ref[...] + change
    spread_rows(jnp.exp2(change), column_ref)
    rows, chunks = plan_ref.shape[0], plan_ref.shape[1] // LANES
    step = 128

    def add_up(b, totals):
        totals = list(totals)
        for row in range(0, step, 16):
            one = pl.ds(pl.multiple_of(b * step + row, 8), 8)
            two = pl.ds(pl.multiple_of(b * step + row + 8, 8), 8)
            for c in range(chunks):
                at = lanes(c)
                plan, plan2 = plan_ref[one, at] * column_ref[one], plan_ref[two, at] * column_ref[two]
                cost = plan * (SCALE - inner_ref[one, at]) + plan2 * (SCALE - inner_ref[two, at])
                totals[c] = totals[c] + (plan + plan2)
                totals[chunks + c] = totals[chunks + c] + cost
        return tuple(totals)

    zero = jnp.zeros((8, LANES), jnp.float32)
    totals = lax.fori_loop(0, rows // step, add_up, (zero,) * (2 * chunks), unroll=2)
    share = LANES // 2
    low = lax.broadcasted_iota(jnp.int32, (1, LANES), 1) < share
    for c in range(chunks):
        plan = jnp.sum(totals[c], axis=0, keepdims=True)
        cost = jnp.sum(totals[chunks + c], axis=0, keepdims=True) * (1.0 / SCALE)
        out_ref[2 * c] = jnp.where(low, plan, pltpu.roll(cost, share, 1))
        out_ref[2 * c + 1] = jnp.where(low, pltpu.roll(plan, share, 1), cost)


def own_half(ref, index):
    line = ref[pl.ds(lax.div(index, 2), 1)]
    share = LANES // 2
    moved = pltpu.roll(line, share, 1)
    return jnp.where(lax.rem(index, 2) == 0, line, moved)[:, :share]


def finish_kernel(log_cols, ratio, sums_ref, phi_ref, gamma_ref, phi_out, gamma_out, reward_out):
    total = sums_ref[0]
    for peer in range(1, sums_ref.shape[0]):
        total = total + sums_ref[peer]
    share = LANES // 2
    plan, cost = total[:, :share], pltpu.roll(total, share, 1)[:, :share]
    phi_out[...] = own_half(phi_ref, lax.axis_index("zh") * 2 + lax.axis_index("core")) * LN2
    spot = lax.axis_index("y") * 8 + lax.axis_index("x") * 2 + lax.axis_index("zl")
    gamma_out[...] = (own_half(gamma_ref, spot) - log_cols - jnp.log2(plan)) * LN2
    reward_out[...] = -ratio * cost / plan


def call(kernel, outs, scratch, *args):
    return pl.pallas_call(
        kernel,
        out_shape=outs,
        in_specs=[VMEM] * len(args),
        out_specs=jax.tree.map(lambda _: VMEM, outs),
        scratch_shapes=scratch,
        compiler_params=PARAMS,
    )(*args)


def body(demo, rollout):
    f32, bf16 = jnp.float32, jnp.bfloat16
    shape = jax.ShapeDtypeStruct
    share, width = demo.shape
    n_plane = lax.axis_size(PLANE)
    n_line, n_sheet = lax.axis_size(LINE), lax.axis_size(SHEET)
    rows, cols = share * n_line, share * n_sheet
    log_rows, log_cols = math.log2(rows * n_sheet), math.log2(cols * n_line)
    row_vec, col_vec = (rows // LANES, LANES), (cols // LANES, LANES)
    tile = shape((rows, cols), f32)
    column = pltpu.VMEM((rows, LANES), f32)

    pair = lax.all_gather(rollout, "zl", axis=0, tiled=True)
    pairs = call(prepare_kernel, shape((n_plane, 2 * share, width), bf16), [], pair)
    rollout_unit = lax.all_to_all(pairs, PLANE, 0, 0, tiled=True).reshape(cols, width)
    demo_unit = lax.all_gather(demo, LINE, axis=0, tiled=True)

    inner, row_parts = call(
        row_lse_kernel,
        (tile, shape((n_line,) + row_vec, f32)),
        [pltpu.VMEM((rows, width), bf16), column, column],
        demo_unit,
        rollout_unit,
    )
    row_parts = lax.all_to_all(row_parts, LINE, 0, 0, tiled=True)
    phi, spread, col_parts = call(
        functools.partial(col_lse_kernel, log_rows),
        (shape(row_vec, f32), shape((rows, LANES), f32), shape((n_sheet,) + col_vec, f32)),
        [pltpu.VMEM(col_vec, f32)],
        row_parts,
        inner,
    )
    col_parts = lax.all_to_all(col_parts, SHEET, 0, 0, tiled=True)
    gamma, plan, row_parts = call(
        functools.partial(row_sum_kernel, log_cols),
        (shape(col_vec, f32), tile, shape((n_line * row_vec[0], LANES), bf16)),
        [column],
        col_parts,
        spread,
        inner,
    )
    row_parts = row_parts.reshape((n_line,) + row_vec)
    row_parts = lax.all_to_all(row_parts, LINE, 0, 0, tiled=True)
    row_parts = row_parts.reshape(n_line * row_vec[0], LANES)
    phi, sums = call(
        functools.partial(col_sum_kernel, log_rows),
        (shape(row_vec, f32), shape((n_sheet, 1, 2 * share), f32)),
        [column],
        row_parts,
        phi,
        plan,
        inner,
    )
    sums = lax.all_to_all(sums, SHEET, 0, 0, tiled=True)
    outs = call(
        functools.partial(finish_kernel, log_cols, 2.0 ** (log_cols - log_rows)),
        (shape((1, share), f32),) * 3,
        [],
        sums,
        phi,
        gamma,
    )
    return tuple(out.reshape(share) for out in outs)


def solution(mesh):
    fine = Mesh(mesh.devices.reshape(8, 2, 2, 4, 4), ALL)
    return jax.shard_map(
        body,
        mesh=fine,
        in_specs=(P(ALL, None), P(ALL, None)),
        out_specs=(P(ALL), P(ALL), P(ALL)),
        check_vma=False,
    )
```

```python
import functools
import math

import jax
import jax.numpy as jnp
from jax import lax
from jax.experimental import pallas as pl
from jax.experimental.pallas import tpu as pltpu
from jax.sharding import Mesh
from jax.sharding import PartitionSpec as P

EPS = 0.005
SCALE = 1.0 / (EPS * math.log(2.0))
LN2 = math.log(2.0)
LANES = 128
CHUNK = 256
PLANE = ("y", "x")
SHEET = ("y", "x", "zl")
LINE = ("zh", "core")
ALL = ("zh", "zl", "core", "y", "x")
VMEM = pl.BlockSpec(memory_space=pltpu.VMEM)
PARAMS = pltpu.CompilerParams(vmem_limit_bytes=6 * 1024 * 1024)


def normalize(embed):
    values = embed.astype(jnp.float32)
    inverse = lax.rsqrt(jnp.sum(values * values, axis=-1, keepdims=True) + 1e-06)
    return (values * inverse).astype(jnp.bfloat16)


def inner_of(left, right):
    return lax.dot_general(
        left, right, (((1,), (1,)), ((), ())), preferred_element_type=jnp.float32
    )


def log_total(parts):
    top = jnp.max(parts, axis=0)
    return top + jnp.log2(jnp.sum(jnp.exp2(parts - top[None]), axis=0))


def lanes(chunk):
    return slice(chunk * LANES, (chunk + 1) * LANES)


def spread_rows(vector, column_ref):
    for block in range(vector.shape[0]):
        wide = jnp.broadcast_to(vector[block : block + 1], (LANES, LANES))
        column_ref[block * LANES : (block + 1) * LANES] = wide.T


def row_lse_kernel(
    raw_ref, raw_rollout_ref, inner_ref, out_ref, demo_ref, rollout_ref, top_ref, total_ref
):
    rows, chunks = inner_ref.shape[0], inner_ref.shape[1] // LANES
    for row in range(0, rows, LANES):
        demo_ref[row : row + LANES] = normalize(raw_ref[row : row + LANES])
    for row in range(0, raw_rollout_ref.shape[0], LANES):
        rollout_ref[row : row + LANES] = normalize(raw_rollout_ref[row : row + LANES])
    for c in range(chunks // 2):
        inner = inner_of(demo_ref[...], rollout_ref[c * CHUNK : (c + 1) * CHUNK]) * SCALE
        inner_ref[:, c * CHUNK : (c + 1) * CHUNK] = inner
        peak = jnp.maximum(inner[:, :LANES], inner[:, LANES:])
        top_ref[...] = peak if c == 0 else jnp.maximum(top_ref[...], peak)

    for row in range(0, rows, 64):
        at = slice(row, row + 64)
        top = top_ref[at]
        total = jnp.zeros_like(top)
        for c in range(chunks):
            total = total + jnp.exp2(inner_ref[at, lanes(c)] - top)
        total_ref[at] = total
    for block in range(rows // LANES):
        at = slice(block * LANES, (block + 1) * LANES)
        top, total = top_ref[at].T, total_ref[at].T
        peak = jnp.max(top, axis=0, keepdims=True)
        total = jnp.sum(total * jnp.exp2(top - peak), axis=0, keepdims=True)
        line = peak - SCALE + jnp.log2(total)
        out_ref[:, block : block + 1] = jnp.broadcast_to(line[None], (out_ref.shape[0], 1, LANES))


def fold(op, values):
    while len(values) > 1:
        values = [op(*pair) for pair in zip(values[::2], values[1::2])]
    return values[0]


def col_lse_kernel(log_rows, parts_ref, inner_ref, phi_ref, column_ref, out_ref, line_ref):
    phi = -log_rows - log_total(parts_ref[...])
    phi_ref[...] = phi
    spread_rows(phi - SCALE, column_ref)
    rows, chunks = inner_ref.shape[0], inner_ref.shape[1] // LANES
    width, strip, strips = 4, 64, 4

    for g in range(chunks // width):

        def some_rows(b, carry, g=g):
            tops, totals = list(carry[:width]), list(carry[width:])
            for s in range(strips):
                expos = [[] for _ in range(width)]
                for row in range(0, strip, 8):
                    at = pl.ds(pl.multiple_of((b * strips + s) * strip + row, 8), 8)
                    column = column_ref[at]
                    for w in range(width):
                        expos[w].append(inner_ref[at, lanes(g * width + w)] + column)
                for w in range(width):
                    top = jnp.maximum(tops[w], fold(jnp.maximum, expos[w]))
                    total = fold(jnp.add, [jnp.exp2(expo - top) for expo in expos[w]])
                    totals[w] = totals[w] * jnp.exp2(tops[w] - top) + total
                    tops[w] = top
            return tuple(tops + totals)

        zero = jnp.zeros((8, LANES), jnp.float32)
        carry = (zero - 1e30,) * width + (zero,) * width
        carry = lax.fori_loop(0, rows // (strip * strips), some_rows, carry, unroll=4)
        for w in range(width):
            peak = jnp.max(carry[w], axis=0, keepdims=True)
            total = carry[width + w] * jnp.exp2(carry[w] - peak)
            total = jnp.sum(total, axis=0, keepdims=True)
            line_ref[g * width + w : g * width + w + 1] = peak + jnp.log2(total)
    out_ref[...] = jnp.broadcast_to(line_ref[...][None], out_ref.shape)


def row_sum_kernel(
    log_cols, parts_ref, column_ref, inner_ref, gamma_ref, plan_ref, out_ref, total_ref
):
    gamma = -log_cols - log_total(parts_ref[...])
    gamma_ref[...] = gamma
    rows, chunks = inner_ref.shape[0], inner_ref.shape[1] // LANES
    for row in range(0, rows, LANES):
        at = slice(row, row + LANES)
        column = column_ref[at]
        total = jnp.zeros_like(column)
        for c in range(chunks):
            plan = jnp.exp2(inner_ref[at, lanes(c)] + (column + gamma[c : c + 1]))
            plan_ref[at, lanes(c)] = plan
            total = total + plan
        total_ref[at] = total
    lines = []
    for block in range(rows // LANES):
        total = total_ref[block * LANES : (block + 1) * LANES].T
        lines.append(jnp.sum(total, axis=0, keepdims=True))
    peers = out_ref.shape[0] // len(lines)
    out_ref[...] = jnp.concatenate(lines * peers).astype(out_ref.dtype)


def col_sum_kernel(
    log_rows, parts_ref, phi_ref, plan_ref, inner_ref, phi_out, out_ref, column_ref
):
    blocks = phi_ref.shape[0]
    parts = parts_ref[...].astype(jnp.float32)
    total = parts[:blocks]
    for peer in range(1, parts.shape[0] // blocks):
        total = total + parts[peer * blocks : (peer + 1) * blocks]
    change = -log_rows - jnp.log2(total)
    phi_out[...] = phi_ref[...] + change
    spread_rows(jnp.exp2(change), column_ref)
    rows, chunks = plan_ref.shape[0], plan_ref.shape[1] // LANES
    step = 128

    def add_up(b, totals):
        totals = list(totals)
        for row in range(0, step, 16):
            one = pl.ds(pl.multiple_of(b * step + row, 8), 8)
            two = pl.ds(pl.multiple_of(b * step + row + 8, 8), 8)
            for c in range(chunks):
                at = lanes(c)
                plan, plan2 = plan_ref[one, at] * column_ref[one], plan_ref[two, at] * column_ref[two]
                cost = plan * (SCALE - inner_ref[one, at]) + plan2 * (SCALE - inner_ref[two, at])
                totals[c] = totals[c] + (plan + plan2)
                totals[chunks + c] = totals[chunks + c] + cost
        return tuple(totals)

    zero = jnp.zeros((8, LANES), jnp.float32)
    totals = lax.fori_loop(0, rows // step, add_up, (zero,) * (2 * chunks), unroll=2)
    share = LANES // 2
    low = lax.broadcasted_iota(jnp.int32, (1, LANES), 1) < share
    for c in range(chunks):
        plan = jnp.sum(totals[c], axis=0, keepdims=True)
        cost = jnp.sum(totals[chunks + c], axis=0, keepdims=True) * (1.0 / SCALE)
        out_ref[2 * c] = jnp.where(low, plan, pltpu.roll(cost, share, 1))
        out_ref[2 * c + 1] = jnp.where(low, pltpu.roll(plan, share, 1), cost)


def own_half(ref, index):
    line = ref[pl.ds(lax.div(index, 2), 1)]
    share = LANES // 2
    moved = pltpu.roll(line, share, 1)
    return jnp.where(lax.rem(index, 2) == 0, line, moved)[:, :share]


def finish_kernel(log_cols, ratio, sums_ref, phi_ref, gamma_ref, phi_out, gamma_out, reward_out):
    total = sums_ref[0]
    for peer in range(1, sums_ref.shape[0]):
        total = total + sums_ref[peer]
    share = LANES // 2
    plan, cost = total[:, :share], pltpu.roll(total, share, 1)[:, :share]
    phi_out[...] = own_half(phi_ref, lax.axis_index("zh") * 2 + lax.axis_index("core")) * LN2
    spot = lax.axis_index("y") * 8 + lax.axis_index("x") * 2 + lax.axis_index("zl")
    gamma_out[...] = (own_half(gamma_ref, spot) - log_cols - jnp.log2(plan)) * LN2
    reward_out[...] = -ratio * cost / plan


def call(kernel, outs, scratch, *args):
    return pl.pallas_call(
        kernel,
        out_shape=outs,
        in_specs=[VMEM] * len(args),
        out_specs=jax.tree.map(lambda _: VMEM, outs),
        scratch_shapes=scratch,
        compiler_params=PARAMS,
    )(*args)


def body(demo, rollout):
    f32, bf16 = jnp.float32, jnp.bfloat16
    shape = jax.ShapeDtypeStruct
    share, width = demo.shape
    n_plane = lax.axis_size(PLANE)
    n_line, n_sheet = lax.axis_size(LINE), lax.axis_size(SHEET)
    rows, cols = share * n_line, share * n_sheet
    log_rows, log_cols = math.log2(rows * n_sheet), math.log2(cols * n_line)
    row_vec, col_vec = (rows // LANES, LANES), (cols // LANES, LANES)
    tile = shape((rows, cols), f32)
    column = pltpu.VMEM((rows, LANES), f32)

    pair = lax.all_gather(rollout, "zl", axis=0, tiled=True)
    pairs = jnp.broadcast_to(pair[None], (n_plane, 2 * share, width))
    rollout_unit = lax.all_to_all(pairs, PLANE, 0, 0, tiled=True).reshape(cols, width)
    demo_unit = lax.all_gather(demo, LINE, axis=0, tiled=True)

    inner, row_parts = call(
        row_lse_kernel,
        (tile, shape((n_line,) + row_vec, f32)),
        [
            pltpu.VMEM((rows, width), bf16),
            pltpu.VMEM((cols, width), bf16),
            column,
            column,
        ],
        demo_unit,
        rollout_unit,
    )
    row_parts = lax.all_to_all(row_parts, LINE, 0, 0, tiled=True)
    phi, spread, col_parts = call(
        functools.partial(col_lse_kernel, log_rows),
        (shape(row_vec, f32), shape((rows, LANES), f32), shape((n_sheet,) + col_vec, f32)),
        [pltpu.VMEM(col_vec, f32)],
        row_parts,
        inner,
    )
    col_parts = lax.all_to_all(col_parts, SHEET[::-1], 0, 0, tiled=True)
    gamma, plan, row_parts = call(
        functools.partial(row_sum_kernel, log_cols),
        (shape(col_vec, f32), tile, shape((n_line * row_vec[0], LANES), bf16)),
        [column],
        col_parts,
        spread,
        inner,
    )
    row_parts = row_parts.reshape((n_line,) + row_vec)
    row_parts = lax.all_to_all(row_parts, LINE, 0, 0, tiled=True)
    row_parts = row_parts.reshape(n_line * row_vec[0], LANES)
    phi, sums = call(
        functools.partial(col_sum_kernel, log_rows),
        (shape(row_vec, f32), shape((n_sheet, 1, 2 * share), f32)),
        [column],
        row_parts,
        phi,
        plan,
        inner,
    )
    sums = lax.all_to_all(sums, SHEET, 0, 0, tiled=True)
    outs = call(
        functools.partial(finish_kernel, log_cols, 2.0 ** (log_cols - log_rows)),
        (shape((1, share), f32),) * 3,
        [],
        sums,
        phi,
        gamma,
    )
    return tuple(out.reshape(share) for out in outs)


def solution(mesh):
    fine = Mesh(mesh.devices.reshape(8, 2, 2, 4, 4), ALL)
    return jax.shard_map(
        body,
        mesh=fine,
        in_specs=(P(ALL, None), P(ALL, None)),
        out_specs=(P(ALL), P(ALL), P(ALL)),
        check_vma=False,
    )
```

```python
import functools
import math

import jax
import jax.numpy as jnp
from jax import lax
from jax.experimental import pallas as pl
from jax.experimental.pallas import tpu as pltpu
from jax.sharding import Mesh
from jax.sharding import PartitionSpec as P

EPS = 0.005
SCALE = 1.0 / (EPS * math.log(2.0))
LN2 = math.log(2.0)
LANES = 128
CHUNK = 512
PLANE = ("y", "x")
SHEET = ("y", "x", "zl")
LINE = ("zh", "core")
ALL = ("zh", "zl", "core", "y", "x")
VMEM = pl.BlockSpec(memory_space=pltpu.VMEM)
PARAMS = pltpu.CompilerParams(vmem_limit_bytes=6 * 1024 * 1024)


def normalize(embed):
    values = embed.astype(jnp.float32)
    inverse = lax.rsqrt(jnp.sum(values * values, axis=-1, keepdims=True) + 1e-06)
    return (values * inverse).astype(jnp.bfloat16)


def inner_of(left, right):
    return lax.dot_general(
        left, right, (((1,), (1,)), ((), ())), preferred_element_type=jnp.float32
    )


def log_total(parts):
    top = jnp.max(parts, axis=0)
    return top + jnp.log2(jnp.sum(jnp.exp2(parts - top[None]), axis=0))


def lanes(chunk):
    return slice(chunk * LANES, (chunk + 1) * LANES)


def spread_rows(vector, column_ref):
    for block in range(vector.shape[0]):
        wide = jnp.broadcast_to(vector[block : block + 1], (LANES, LANES))
        column_ref[block * LANES : (block + 1) * LANES] = wide.T


def row_lse_kernel(
    raw_ref, raw_rollout_ref, inner_ref, out_ref, demo_ref, rollout_ref, top_ref, total_ref
):
    rows, chunks = inner_ref.shape[0], inner_ref.shape[1] // LANES
    for row in range(0, rows, LANES):
        demo_ref[row : row + LANES] = normalize(raw_ref[row : row + LANES])
    for row in range(0, raw_rollout_ref.shape[0], LANES):
        rollout_ref[row : row + LANES] = normalize(raw_rollout_ref[row : row + LANES])
    for c in range(chunks * LANES // CHUNK):
        inner = inner_of(demo_ref[...], rollout_ref[c * CHUNK : (c + 1) * CHUNK]) * SCALE
        inner_ref[:, c * CHUNK : (c + 1) * CHUNK] = inner
        peak = fold(jnp.maximum, [inner[:, lanes(k)] for k in range(CHUNK // LANES)])
        top_ref[...] = peak if c == 0 else jnp.maximum(top_ref[...], peak)

    for row in range(0, rows, 64):
        at = slice(row, row + 64)
        top = top_ref[at]
        total = jnp.zeros_like(top)
        for c in range(chunks):
            total = total + jnp.exp2(inner_ref[at, lanes(c)] - top)
        total_ref[at] = total
    for block in range(rows // LANES):
        at = slice(block * LANES, (block + 1) * LANES)
        top, total = top_ref[at].T, total_ref[at].T
        peak = jnp.max(top, axis=0, keepdims=True)
        total = jnp.sum(total * jnp.exp2(top - peak), axis=0, keepdims=True)
        line = peak - SCALE + jnp.log2(total)
        out_ref[:, block : block + 1] = jnp.broadcast_to(line[None], (out_ref.shape[0], 1, LANES))


def fold(op, values):
    while len(values) > 1:
        values = [op(*pair) for pair in zip(values[::2], values[1::2])]
    return values[0]


def col_lse_kernel(log_rows, parts_ref, inner_ref, phi_ref, column_ref, out_ref, line_ref):
    phi = -log_rows - log_total(parts_ref[...])
    phi_ref[...] = phi
    spread_rows(phi - SCALE, column_ref)
    rows, chunks = inner_ref.shape[0], inner_ref.shape[1] // LANES
    width, strip, strips = 4, 64, 4

    for g in range(chunks // width):

        def some_rows(b, carry, g=g):
            tops, totals = list(carry[:width]), list(carry[width:])
            for s in range(strips):
                expos = [[] for _ in range(width)]
                for row in range(0, strip, 8):
                    at = pl.ds(pl.multiple_of((b * strips + s) * strip + row, 8), 8)
                    column = column_ref[at]
                    for w in range(width):
                        expos[w].append(inner_ref[at, lanes(g * width + w)] + column)
                for w in range(width):
                    top = jnp.maximum(tops[w], fold(jnp.maximum, expos[w]))
                    total = fold(jnp.add, [jnp.exp2(expo - top) for expo in expos[w]])
                    totals[w] = totals[w] * jnp.exp2(tops[w] - top) + total
                    tops[w] = top
            return tuple(tops + totals)

        zero = jnp.zeros((8, LANES), jnp.float32)
        carry = (zero - 1e30,) * width + (zero,) * width
        carry = lax.fori_loop(0, rows // (strip * strips), some_rows, carry, unroll=4)
        for w in range(width):
            peak = jnp.max(carry[w], axis=0, keepdims=True)
            total = carry[width + w] * jnp.exp2(carry[w] - peak)
            total = jnp.sum(total, axis=0, keepdims=True)
            line_ref[g * width + w : g * width + w + 1] = peak + jnp.log2(total)
    out_ref[...] = jnp.broadcast_to(line_ref[...][None], out_ref.shape)


def row_sum_kernel(
    log_cols, parts_ref, column_ref, inner_ref, gamma_ref, plan_ref, out_ref, total_ref
):
    gamma = -log_cols - log_total(parts_ref[...])
    gamma_ref[...] = gamma
    rows, chunks = inner_ref.shape[0], inner_ref.shape[1] // LANES
    for row in range(0, rows, LANES):
        at = slice(row, row + LANES)
        column = column_ref[at]
        total = jnp.zeros_like(column)
        for c in range(chunks):
            plan = jnp.exp2(inner_ref[at, lanes(c)] + (column + gamma[c : c + 1]))
            plan_ref[at, lanes(c)] = plan
            total = total + plan
        total_ref[at] = total
    lines = []
    for block in range(rows // LANES):
        total = total_ref[block * LANES : (block + 1) * LANES].T
        lines.append(jnp.sum(total, axis=0, keepdims=True))
    peers = out_ref.shape[0] // len(lines)
    out_ref[...] = jnp.concatenate(lines * peers).astype(out_ref.dtype)


def col_sum_kernel(
    log_rows, parts_ref, phi_ref, plan_ref, inner_ref, phi_out, out_ref, column_ref
):
    blocks = phi_ref.shape[0]
    parts = parts_ref[...].astype(jnp.float32)
    total = parts[:blocks]
    for peer in range(1, parts.shape[0] // blocks):
        total = total + parts[peer * blocks : (peer + 1) * blocks]
    change = -log_rows - jnp.log2(total)
    phi_out[...] = phi_ref[...] + change
    spread_rows(jnp.exp2(change), column_ref)
    rows, chunks = plan_ref.shape[0], plan_ref.shape[1] // LANES
    step = 128

    def add_up(b, totals):
        totals = list(totals)
        for row in range(0, step, 16):
            one = pl.ds(pl.multiple_of(b * step + row, 8), 8)
            two = pl.ds(pl.multiple_of(b * step + row + 8, 8), 8)
            for c in range(chunks):
                at = lanes(c)
                plan, plan2 = plan_ref[one, at] * column_ref[one], plan_ref[two, at] * column_ref[two]
                cost = plan * (SCALE - inner_ref[one, at]) + plan2 * (SCALE - inner_ref[two, at])
                totals[c] = totals[c] + (plan + plan2)
                totals[chunks + c] = totals[chunks + c] + cost
        return tuple(totals)

    zero = jnp.zeros((8, LANES), jnp.float32)
    totals = lax.fori_loop(0, rows // step, add_up, (zero,) * (2 * chunks), unroll=2)
    share = LANES // 2
    low = lax.broadcasted_iota(jnp.int32, (1, LANES), 1) < share
    for c in range(chunks):
        plan = jnp.sum(totals[c], axis=0, keepdims=True)
        cost = jnp.sum(totals[chunks + c], axis=0, keepdims=True) * (1.0 / SCALE)
        out_ref[2 * c] = jnp.where(low, plan, pltpu.roll(cost, share, 1))
        out_ref[2 * c + 1] = jnp.where(low, pltpu.roll(plan, share, 1), cost)


def own_half(ref, index):
    line = ref[pl.ds(lax.div(index, 2), 1)]
    share = LANES // 2
    moved = pltpu.roll(line, share, 1)
    return jnp.where(lax.rem(index, 2) == 0, line, moved)[:, :share]


def finish_kernel(log_cols, ratio, sums_ref, phi_ref, gamma_ref, phi_out, gamma_out, reward_out):
    total = sums_ref[0]
    for peer in range(1, sums_ref.shape[0]):
        total = total + sums_ref[peer]
    share = LANES // 2
    plan, cost = total[:, :share], pltpu.roll(total, share, 1)[:, :share]
    phi_out[...] = own_half(phi_ref, lax.axis_index("zh") * 2 + lax.axis_index("core")) * LN2
    spot = lax.axis_index("y") * 8 + lax.axis_index("x") * 2 + lax.axis_index("zl")
    gamma_out[...] = (own_half(gamma_ref, spot) - log_cols - jnp.log2(plan)) * LN2
    reward_out[...] = -ratio * cost / plan


def call(kernel, outs, scratch, *args):
    return pl.pallas_call(
        kernel,
        out_shape=outs,
        in_specs=[VMEM] * len(args),
        out_specs=jax.tree.map(lambda _: VMEM, outs),
        scratch_shapes=scratch,
        compiler_params=PARAMS,
    )(*args)


def body(demo, rollout):
    f32, bf16 = jnp.float32, jnp.bfloat16
    shape = jax.ShapeDtypeStruct
    share, width = demo.shape
    n_plane = lax.axis_size(PLANE)
    n_line, n_sheet = lax.axis_size(LINE), lax.axis_size(SHEET)
    rows, cols = share * n_line, share * n_sheet
    log_rows, log_cols = math.log2(rows * n_sheet), math.log2(cols * n_line)
    row_vec, col_vec = (rows // LANES, LANES), (cols // LANES, LANES)
    tile = shape((rows, cols), f32)
    column = pltpu.VMEM((rows, LANES), f32)

    pair = lax.all_gather(rollout, "zl", axis=0, tiled=True)
    pairs = jnp.broadcast_to(pair[None], (n_plane, 2 * share, width))
    rollout_unit = lax.all_to_all(pairs, PLANE, 0, 0, tiled=True).reshape(cols, width)
    demo_unit = lax.all_gather(demo, LINE, axis=0, tiled=True)

    inner, row_parts = call(
        row_lse_kernel,
        (tile, shape((n_line,) + row_vec, f32)),
        [
            pltpu.VMEM((rows, width), bf16),
            pltpu.VMEM((cols, width), bf16),
            column,
            column,
        ],
        demo_unit,
        rollout_unit,
    )
    row_parts = lax.all_to_all(row_parts, LINE, 0, 0, tiled=True)
    phi, spread, col_parts = call(
        functools.partial(col_lse_kernel, log_rows),
        (shape(row_vec, f32), shape((rows, LANES), f32), shape((n_sheet,) + col_vec, f32)),
        [pltpu.VMEM(col_vec, f32)],
        row_parts,
        inner,
    )
    col_parts = lax.all_to_all(col_parts, SHEET[::-1], 0, 0, tiled=True)
    gamma, plan, row_parts = call(
        functools.partial(row_sum_kernel, log_cols),
        (shape(col_vec, f32), tile, shape((n_line * row_vec[0], LANES), bf16)),
        [column],
        col_parts,
        spread,
        inner,
    )
    row_parts = row_parts.reshape((n_line,) + row_vec)
    row_parts = lax.all_to_all(row_parts, LINE, 0, 0, tiled=True)
    row_parts = row_parts.reshape(n_line * row_vec[0], LANES)
    phi, sums = call(
        functools.partial(col_sum_kernel, log_rows),
        (shape(row_vec, f32), shape((n_sheet, 1, 2 * share), f32)),
        [column],
        row_parts,
        phi,
        plan,
        inner,
    )
    sums = lax.all_to_all(sums, SHEET, 0, 0, tiled=True)
    outs = call(
        functools.partial(finish_kernel, log_cols, 2.0 ** (log_cols - log_rows)),
        (shape((1, share), f32),) * 3,
        [],
        sums,
        phi,
        gamma,
    )
    return tuple(out.reshape(share) for out in outs)


def solution(mesh):
    fine = Mesh(mesh.devices.reshape(8, 2, 2, 4, 4), ALL)
    return jax.shard_map(
        body,
        mesh=fine,
        in_specs=(P(ALL, None), P(ALL, None)),
        out_specs=(P(ALL), P(ALL), P(ALL)),
        check_vma=False,
    )
```

```python
import functools
import math

import jax
import jax.numpy as jnp
from jax import lax
from jax.experimental import pallas as pl
from jax.experimental.pallas import tpu as pltpu
from jax.sharding import Mesh
from jax.sharding import PartitionSpec as P

EPS = 0.005
SCALE = 1.0 / (EPS * math.log(2.0))
LN2 = math.log(2.0)
LANES = 128
CHUNK = 256
PLANE = ("y", "x")
SHEET = ("y", "x", "zl")
LINE = ("zh", "core")
ALL = ("zh", "zl", "core", "y", "x")
VMEM = pl.BlockSpec(memory_space=pltpu.VMEM)
PARAMS = pltpu.CompilerParams(vmem_limit_bytes=6 * 1024 * 1024)


def normalize(embed):
    values = embed.astype(jnp.float32)
    inverse = lax.rsqrt(jnp.sum(values * values, axis=-1, keepdims=True) + 1e-06)
    return (values * inverse).astype(jnp.bfloat16)


def inner_of(left, right):
    return lax.dot_general(
        left, right, (((1,), (1,)), ((), ())), preferred_element_type=jnp.float32
    )


def log_total(parts):
    top = jnp.max(parts, axis=0)
    return top + jnp.log2(jnp.sum(jnp.exp2(parts - top[None]), axis=0))


def lanes(chunk):
    return slice(chunk * LANES, (chunk + 1) * LANES)


def spread_rows(vector, column_ref):
    for block in range(vector.shape[0]):
        wide = jnp.broadcast_to(vector[block : block + 1], (LANES, LANES))
        column_ref[block * LANES : (block + 1) * LANES] = wide.T


def row_lse_kernel(
    raw_ref, raw_rollout_ref, inner_ref, out_ref, demo_ref, rollout_ref, top_ref, total_ref
):
    rows, chunks = inner_ref.shape[0], inner_ref.shape[1] // LANES
    for row in range(0, rows, LANES):
        demo_ref[row : row + LANES] = normalize(raw_ref[row : row + LANES])
    for row in range(0, raw_rollout_ref.shape[0], LANES):
        rollout_ref[row : row + LANES] = normalize(raw_rollout_ref[row : row + LANES])
    for c in range(chunks // 2):
        inner = inner_of(demo_ref[...], rollout_ref[c * CHUNK : (c + 1) * CHUNK]) * SCALE
        inner_ref[:, c * CHUNK : (c + 1) * CHUNK] = inner
        peak = jnp.maximum(inner[:, :LANES], inner[:, LANES:])
        top_ref[...] = peak if c == 0 else jnp.maximum(top_ref[...], peak)

    for row in range(0, rows, 64):
        at = slice(row, row + 64)
        top = top_ref[at]
        total = jnp.zeros_like(top)
        for c in range(chunks):
            total = total + jnp.exp2(inner_ref[at, lanes(c)] - top)
        total_ref[at] = total
    for block in range(rows // LANES):
        at = slice(block * LANES, (block + 1) * LANES)
        top, total = top_ref[at].T, total_ref[at].T
        peak = jnp.max(top, axis=0, keepdims=True)
        total = jnp.sum(total * jnp.exp2(top - peak), axis=0, keepdims=True)
        line = peak - SCALE + jnp.log2(total)
        out_ref[:, block : block + 1] = jnp.broadcast_to(line[None], (out_ref.shape[0], 1, LANES))


def fold(op, values):
    while len(values) > 1:
        values = [op(*pair) for pair in zip(values[::2], values[1::2])]
    return values[0]


def col_lse_kernel(log_rows, parts_ref, inner_ref, phi_ref, column_ref, out_ref, line_ref):
    phi = -log_rows - log_total(parts_ref[...])
    phi_ref[...] = phi
    spread_rows(phi - SCALE, column_ref)
    rows, chunks = inner_ref.shape[0], inner_ref.shape[1] // LANES
    width, strip, strips = 4, 64, 4

    for g in range(chunks // width):

        def some_rows(b, carry, g=g):
            tops, totals = list(carry[:width]), list(carry[width:])
            for s in range(strips):
                expos = [[] for _ in range(width)]
                for row in range(0, strip, 8):
                    at = pl.ds(pl.multiple_of((b * strips + s) * strip + row, 8), 8)
                    column = column_ref[at]
                    for w in range(width):
                        expos[w].append(inner_ref[at, lanes(g * width + w)] + column)
                for w in range(width):
                    top = jnp.maximum(tops[w], fold(jnp.maximum, expos[w]))
                    total = fold(jnp.add, [jnp.exp2(expo - top) for expo in expos[w]])
                    totals[w] = totals[w] * jnp.exp2(tops[w] - top) + total
                    tops[w] = top
            return tuple(tops + totals)

        zero = jnp.zeros((8, LANES), jnp.float32)
        carry = (zero - 1e30,) * width + (zero,) * width
        carry = lax.fori_loop(0, rows // (strip * strips), some_rows, carry, unroll=4)
        for w in range(width):
            peak = jnp.max(carry[w], axis=0, keepdims=True)
            total = carry[width + w] * jnp.exp2(carry[w] - peak)
            total = jnp.sum(total, axis=0, keepdims=True)
            line_ref[g * width + w : g * width + w + 1] = peak + jnp.log2(total)
    out_ref[...] = jnp.broadcast_to(line_ref[...][None], out_ref.shape)


def row_sum_kernel(
    log_cols, parts_ref, column_ref, inner_ref, gamma_ref, plan_ref, out_ref, total_ref
):
    gamma = -log_cols - log_total(parts_ref[...])
    gamma_ref[...] = gamma
    rows, chunks = inner_ref.shape[0], inner_ref.shape[1] // LANES
    for row in range(0, rows, LANES):
        at = slice(row, row + LANES)
        column = column_ref[at]
        total = jnp.zeros_like(column)
        for c in range(chunks):
            plan = jnp.exp2(inner_ref[at, lanes(c)] + (column + gamma[c : c + 1]))
            plan_ref[at, lanes(c)] = plan
            total = total + plan
        total_ref[at] = total
    lines = []
    for block in range(rows // LANES):
        total = total_ref[block * LANES : (block + 1) * LANES].T
        lines.append(jnp.sum(total, axis=0, keepdims=True))
    peers = out_ref.shape[0] // len(lines)
    out_ref[...] = jnp.concatenate(lines * peers).astype(out_ref.dtype)


def col_sum_kernel(
    log_rows, parts_ref, phi_ref, plan_ref, inner_ref, phi_out, out_ref, column_ref
):
    blocks = phi_ref.shape[0]
    parts = parts_ref[...].astype(jnp.float32)
    total = parts[:blocks]
    for peer in range(1, parts.shape[0] // blocks):
        total = total + parts[peer * blocks : (peer + 1) * blocks]
    change = -log_rows - jnp.log2(total)
    phi_out[...] = phi_ref[...] + change
    spread_rows(jnp.exp2(change), column_ref)
    rows, chunks = plan_ref.shape[0], plan_ref.shape[1] // LANES
    step = 256

    def add_up(b, totals):
        totals = list(totals)
        for row in range(0, step, 16):
            one = pl.ds(pl.multiple_of(b * step + row, 8), 8)
            two = pl.ds(pl.multiple_of(b * step + row + 8, 8), 8)
            for c in range(chunks):
                at = lanes(c)
                plan, plan2 = plan_ref[one, at] * column_ref[one], plan_ref[two, at] * column_ref[two]
                cost = plan * (SCALE - inner_ref[one, at]) + plan2 * (SCALE - inner_ref[two, at])
                totals[c] = totals[c] + (plan + plan2)
                totals[chunks + c] = totals[chunks + c] + cost
        return tuple(totals)

    zero = jnp.zeros((8, LANES), jnp.float32)
    totals = lax.fori_loop(0, rows // step, add_up, (zero,) * (2 * chunks), unroll=2)
    share = LANES // 2
    low = lax.broadcasted_iota(jnp.int32, (1, LANES), 1) < share
    for c in range(chunks):
        plan = jnp.sum(totals[c], axis=0, keepdims=True)
        cost = jnp.sum(totals[chunks + c], axis=0, keepdims=True) * (1.0 / SCALE)
        out_ref[2 * c] = jnp.where(low, plan, pltpu.roll(cost, share, 1))
        out_ref[2 * c + 1] = jnp.where(low, pltpu.roll(plan, share, 1), cost)


def own_half(ref, index):
    line = ref[pl.ds(lax.div(index, 2), 1)]
    share = LANES // 2
    moved = pltpu.roll(line, share, 1)
    return jnp.where(lax.rem(index, 2) == 0, line, moved)[:, :share]


def finish_kernel(log_cols, ratio, sums_ref, phi_ref, gamma_ref, phi_out, gamma_out, reward_out):
    total = sums_ref[0]
    for peer in range(1, sums_ref.shape[0]):
        total = total + sums_ref[peer]
    share = LANES // 2
    plan, cost = total[:, :share], pltpu.roll(total, share, 1)[:, :share]
    phi_out[...] = own_half(phi_ref, lax.axis_index("zh") * 2 + lax.axis_index("core")) * LN2
    spot = lax.axis_index("y") * 8 + lax.axis_index("x") * 2 + lax.axis_index("zl")
    gamma_out[...] = (own_half(gamma_ref, spot) - log_cols - jnp.log2(plan)) * LN2
    reward_out[...] = -ratio * cost / plan


def call(kernel, outs, scratch, *args):
    return pl.pallas_call(
        kernel,
        out_shape=outs,
        in_specs=[VMEM] * len(args),
        out_specs=jax.tree.map(lambda _: VMEM, outs),
        scratch_shapes=scratch,
        compiler_params=PARAMS,
    )(*args)


def body(demo, rollout):
    f32, bf16 = jnp.float32, jnp.bfloat16
    shape = jax.ShapeDtypeStruct
    share, width = demo.shape
    n_plane = lax.axis_size(PLANE)
    n_line, n_sheet = lax.axis_size(LINE), lax.axis_size(SHEET)
    rows, cols = share * n_line, share * n_sheet
    log_rows, log_cols = math.log2(rows * n_sheet), math.log2(cols * n_line)
    row_vec, col_vec = (rows // LANES, LANES), (cols // LANES, LANES)
    tile = shape((rows, cols), f32)
    column = pltpu.VMEM((rows, LANES), f32)

    pair = lax.all_gather(rollout, "zl", axis=0, tiled=True)
    pairs = jnp.broadcast_to(pair[None], (n_plane, 2 * share, width))
    rollout_unit = lax.all_to_all(pairs, PLANE, 0, 0, tiled=True).reshape(cols, width)
    demo_unit = lax.all_gather(demo, LINE, axis=0, tiled=True)

    inner, row_parts = call(
        row_lse_kernel,
        (tile, shape((n_line,) + row_vec, f32)),
        [
            pltpu.VMEM((rows, width), bf16),
            pltpu.VMEM((cols, width), bf16),
            column,
            column,
        ],
        demo_unit,
        rollout_unit,
    )
    row_parts = lax.all_to_all(row_parts, LINE, 0, 0, tiled=True)
    phi, spread, col_parts = call(
        functools.partial(col_lse_kernel, log_rows),
        (shape(row_vec, f32), shape((rows, LANES), f32), shape((n_sheet,) + col_vec, f32)),
        [pltpu.VMEM(col_vec, f32)],
        row_parts,
        inner,
    )
    col_parts = lax.all_to_all(col_parts, SHEET[::-1], 0, 0, tiled=True)
    gamma, plan, row_parts = call(
        functools.partial(row_sum_kernel, log_cols),
        (shape(col_vec, f32), tile, shape((n_line * row_vec[0], LANES), bf16)),
        [column],
        col_parts,
        spread,
        inner,
    )
    row_parts = row_parts.reshape((n_line,) + row_vec)
    row_parts = lax.all_to_all(row_parts, LINE, 0, 0, tiled=True)
    row_parts = row_parts.reshape(n_line * row_vec[0], LANES)
    phi, sums = call(
        functools.partial(col_sum_kernel, log_rows),
        (shape(row_vec, f32), shape((n_sheet, 1, 2 * share), f32)),
        [column],
        row_parts,
        phi,
        plan,
        inner,
    )
    sums = lax.all_to_all(sums, SHEET, 0, 0, tiled=True)
    outs = call(
        functools.partial(finish_kernel, log_cols, 2.0 ** (log_cols - log_rows)),
        (shape((1, share), f32),) * 3,
        [],
        sums,
        phi,
        gamma,
    )
    return tuple(out.reshape(share) for out in outs)


def solution(mesh):
    fine = Mesh(mesh.devices.reshape(8, 2, 2, 4, 4), ALL)
    return jax.shard_map(
        body,
        mesh=fine,
        in_specs=(P(ALL, None), P(ALL, None)),
        out_specs=(P(ALL), P(ALL), P(ALL)),
        check_vma=False,
    )
```
